32 devices in a mesh: dp: 4 (over y, core), expert: 8 (over z, x).
Axes of the slice: x: 2, y: 2, z: 4, core: 2. Of those that a mesh axis runs over, the one named last changes fastest.
Arguments:
- cotangent: bfloat16 [4096, 2048], P(('dp', 'expert')), may hold values from -6 to 6
- gate_prob: bfloat16 [4096, 8], P(('dp', 'expert')), may hold values from 0.029907227 to 0.3984375
- routes: int32 [4096, 8], P(('dp', 'expert')), may hold values from 0 to 15, all different within a row; in each aligned block of 128 rows (0 to 127, 128 to 255, ...) at most 96 rows name the same one
- hidden: bfloat16 [4, 16, 8, 96, 768], P('dp', 'expert'), may hold values from -0.3984375 to 0.3984375
- down_weight: bfloat16 [16, 768, 2048], P('expert'), may hold values from -0.21875 to 0.21875
- sign_seed: int32 [2048], replicated, may hold values from 0 to 1
Outputs:
- grad_hidden: bfloat16 [4, 16, 8, 96, 768], P('dp', 'expert')
- grad_prob: float32 [4096, 8], P(('dp', 'expert'))
- grad_weight: float32 [2048, 16, 768], P('dp', 'expert')
The draws below stay inside these ranges and needn't reach their ends.
Inputs may be any that keep to these rules, and one draw needn't show every extreme that they name: `routes`: each row names 8 different experts; in each device's block of 128 tokens no expert is named by more than 96 tokens, and in some block one expert is named by exactly 96.
All inputs are finite; a program needn't handle non-finite values.
Results may differ from the reference program's by a relative error of at most 0.015.
Values may be sent and summed in bfloat16 or wider, within the bound.
No kernel may reach another device: no remote copies, remote signals or barrier semaphores. Data moves between devices by JAX's collectives and lax.ppermute only.
A program may use at most 128 MiB of HBM per device.

```python
import math
import jax
import jax.numpy as jnp
import numpy as np
from jax import lax

D = 2048
FF = 768
TOPK = 8
BLOCK = 128
TOK_DEV = 128
GROUPS = 4
SOURCES = 8
EXPERTS = 16
TOKENS = 4096
CAP = 96


def touch_ends(array, stream_key, least, largest):
    shape = array.shape
    index_at = [jax.random.randint(jax.random.fold_in(stream_key, axis), (), 0, shape[axis]) for axis in range(len(shape))]
    array = array.at[tuple(index_at)].set(least)
    longest = shape.index(max(shape))
    index_at[longest] = (index_at[longest] + 1) % shape[longest]
    return array.at[tuple(index_at)].set(largest)


def steps_of(stream_key, shape, shards, smallest, largest):
    level, own = 1.0, jax.random.fold_in(stream_key, 6)
    for axis_at, blocks in shards:
        draws = jnp.exp(jax.random.uniform(jax.random.fold_in(own, axis_at), (blocks,), jnp.float32, smallest / len(shards), largest / len(shards)))
        level = level * jnp.repeat(draws, shape[axis_at] // blocks).reshape([-1 if axis == axis_at else 1 for axis in range(len(shape))])
    return level


def routed_block(own_key, own, number, rows, count, top, most, skew):
    order = jax.random.permutation(own_key, count)
    crowded, ordinary = portions_of(count, rows * top, most, skew, True), portions_of(count, rows * top, most, skew, False)
    places = jnp.arange(count)

    def named(tallies, turn):
        used = int((tallies > 0).sum())
        fixed = max(1, used // 4)
        passed = fixed + (places - fixed + turn * (used - fixed)) % max(1, count - fixed)
        return jnp.zeros((count,), jnp.int32).at[order[jnp.where(places < fixed, places, passed)]].set(jnp.asarray(tallies, jnp.int32))

    tallies = jnp.where(number % 4 == 0, named(crowded, number // 4), named(ordinary, number - number // 4 - 1))
    mixed = jax.random.permutation(jax.random.fold_in(own, 3), count)
    source_of, taker = mixed[0:count // 2 * 2:2], mixed[1:count // 2 * 2:2]
    room = jnp.minimum(tallies[source_of] - 1, most - tallies[taker]) // 2
    room = jnp.where((source_of == order[0]) | (taker == order[0]) | (tallies[taker] == 0), 0, jnp.maximum(room, 0))
    passed = jax.random.randint(jax.random.fold_in(own, 4), (count // 2,), 0, 1 << 20) % (room + 1)
    tallies = tallies.at[source_of].add(-passed).at[taker].add(passed)
    labels = jnp.searchsorted(jnp.cumsum(tallies), jnp.arange(rows * top), side="right").astype(jnp.int32)
    grid = labels.reshape(top, rows).T
    grid = grid[jax.random.permutation(jax.random.fold_in(own, 1), rows)]
    turn = jax.random.randint(jax.random.fold_in(own, 2), (rows, 1), 0, top)
    return jnp.take_along_axis(grid, (jnp.arange(top)[None, :] + turn) % top, axis=1)


def portions_of(count, total, limit, lean, full):
    loads = [(1 << 20) // math.isqrt(standing ** lean) + 1 for standing in range(1, count + 1)]
    largest = limit if full else min(limit, max(-(-total // count), total * loads[0] // sum(loads)))
    least = 1 if total - largest >= count - 1 else 0
    given, spare = [largest] + [least] * (count - 1), total - largest - least * (count - 1)
    while spare > 0:
        free = [i for i in range(1, count) if given[i] < largest] or [i for i in range(1, count) if given[i] < limit]
        mass, left = sum([loads[i] for i in free]), spare
        for i in free:
            extra = min(limit - given[i], max(1, left * loads[i] // mass), spare)
            given[i] = given[i] + extra
            spare = spare - extra
    return np.array(given)


def normal_values(key, shape, scale, limit, cuts=(), kind=jnp.bfloat16):
    array = scale * jax.random.normal(key, shape, jnp.float32)
    if cuts:
        array = array * steps_of(key, shape, cuts, -0.22, 0.18)
    return jnp.clip(array, -limit, limit).astype(kind)


def setup_inputs(seed: int = 0) -> dict:
    arg_keys = jax.random.split(jax.random.key(seed), 7)
    cotangent = normal_values(arg_keys[0], (TOKENS, D), 1.0, 6.0, ((0, 32),))
    gate_prob = jnp.clip(jnp.exp(math.log(0.3984375) - 2.5894505 * jax.random.uniform(arg_keys[1], (TOKENS, TOPK), jnp.float32) ** steps_of(arg_keys[1], (TOKENS, TOPK), ((0, 32),), -0.2, 0.2)), 0.029907227, 0.3984375).astype(jnp.bfloat16)
    routes_keys = jax.random.split(jax.random.fold_in(arg_keys[2], 1), TOKENS // TOK_DEV)
    routes_turns = jax.random.permutation(jax.random.fold_in(arg_keys[2], 3), TOKENS // TOK_DEV)
    routes = jax.vmap(lambda own, number: routed_block(jax.random.fold_in(arg_keys[2], 2), own, number, TOK_DEV, EXPERTS, TOPK, CAP, 2))(routes_keys, routes_turns).reshape((TOKENS, TOPK))
    hidden = normal_values(arg_keys[3], (GROUPS, EXPERTS, SOURCES, CAP, FF), 0.05, 0.3984375, ((0, 4), (1, 8)))
    down_weight = normal_values(arg_keys[4], (EXPERTS, FF, D), FF ** -0.5, 0.21875, ((0, 8),))
    sign_seed = touch_ends(jax.random.randint(arg_keys[5], (D,), 0, 2), jax.random.fold_in(arg_keys[5], 1), 0, 1).astype(jnp.int32)
    return {"cotangent": cotangent, "gate_prob": gate_prob, "routes": routes, "hidden": hidden, "down_weight": down_weight, "sign_seed": sign_seed}


def hadamard(length):
    index_vec = jnp.arange(length, dtype=jnp.int32)
    anded = jnp.bitwise_and(index_vec[:, None], index_vec[None, :])
    parity = jnp.zeros((length, length), jnp.int32)
    for shift_by in range(max(length.bit_length() - 1, 1)):
        parity = parity + jnp.bitwise_and(jnp.right_shift(anded, shift_by), 1)
    return (1.0 - 2.0 * (parity % 2).astype(jnp.float32)) / math.sqrt(length)

def block_slots(routes, experts_all):
    hit_count = lax.optimization_barrier(jnp.sum((routes[:, :, None] == jnp.arange(experts_all, dtype=jnp.int32)).astype(jnp.int32), axis=1, dtype=jnp.int32))
    before = jnp.cumsum(hit_count, axis=0, dtype=jnp.int32) - hit_count
    return jnp.take_along_axis(before, routes, axis=1)

def reference(cotangent, gate_prob, routes, hidden, down_weight, sign_seed):
    block_total = GROUPS * SOURCES
    blocks = routes.reshape(block_total, TOK_DEV, TOPK)
    slot_rank = jax.vmap(block_slots, in_axes=(0, None))(blocks, EXPERTS)
    block_id = jnp.arange(block_total, dtype=jnp.int32)[:, None, None]
    group = block_id // SOURCES
    source = block_id % SOURCES
    position = ((blocks * GROUPS + group) * SOURCES + source) * CAP + slot_rank
    pair_count = TOKENS * TOPK
    pair_table = jnp.full((EXPERTS * GROUPS * SOURCES * CAP,), pair_count, jnp.int32)
    pair_table = pair_table.at[position.reshape(-1)].set(jnp.arange(pair_count, dtype=jnp.int32))
    pair_table = pair_table.reshape(EXPERTS, GROUPS, SOURCES, CAP)
    sign_vec = (2 * sign_seed - 1).astype(jnp.float32)
    rotation = hadamard(BLOCK)
    flat_gate = gate_prob.reshape(-1)

    def per_expert(expert):
        slot_table = lax.dynamic_index_in_dim(pair_table, expert, 0, keepdims=False).reshape(-1)
        routed_rows = jnp.take(cotangent, slot_table // TOPK, axis=0, mode='fill', fill_value=0)
        weights_here = jnp.take(flat_gate, slot_table, axis=0, mode='fill', fill_value=0).astype(jnp.float32)[:, None]
        saved_rows = lax.dynamic_index_in_dim(hidden, expert, 1, keepdims=False).reshape(-1, FF)
        weight = lax.dynamic_index_in_dim(down_weight, expert, 0, keepdims=False)
        back_grad = jnp.dot(routed_rows, weight.T, preferred_element_type=jnp.float32)
        hidden_grad = (weights_here * back_grad).astype(jnp.bfloat16)
        slot_grad = lax.optimization_barrier(jnp.sum(back_grad * saved_rows.astype(jnp.float32), axis=1))
        weighted = (weights_here * saved_rows.astype(jnp.float32)).astype(jnp.bfloat16)
        per_group = jnp.einsum('gxd,gxf->gdf', routed_rows.reshape(GROUPS, -1, D).astype(jnp.float32), weighted.reshape(GROUPS, -1, FF).astype(jnp.float32))
        shaped = per_group.reshape(GROUPS, D // BLOCK, BLOCK, FF) * sign_vec.reshape(1, D // BLOCK, BLOCK, 1)
        turned = jnp.einsum('ij,gbjf->gbif', rotation, shaped, precision=lax.Precision.HIGHEST)
        rounded = lax.optimization_barrier(turned.astype(jnp.bfloat16)).astype(jnp.float32)
        summed = lax.optimization_barrier(jnp.sum(rounded, axis=0)).reshape(D, FF)
        return (hidden_grad.reshape(GROUPS, SOURCES, CAP, FF), slot_grad, summed)
    hidden_grad, slot_grad, summed = lax.map(per_expert, jnp.arange(EXPERTS, dtype=jnp.int32))
    grad_hidden = jnp.transpose(hidden_grad, (1, 0, 2, 3, 4))
    grad_prob = slot_grad.reshape(-1)[position.reshape(-1)].reshape(TOKENS, TOPK)
    grad_weight = jnp.transpose(summed, (1, 0, 2))
    return (grad_hidden, grad_prob, grad_weight)
```

```python
import functools
import math

import jax
import jax.numpy as jnp
from jax import lax
from jax.experimental import pallas as pl
from jax.experimental.pallas import tpu as pltpu
from jax.sharding import PartitionSpec as P

BLOCK = 128
LANES = 128
CORES = 2
NO_SLOT = 512.0
VMEM = 56 * 1024 * 1024
F32 = jnp.float32
BF16 = jnp.bfloat16


ANY = pl.BlockSpec(memory_space=pl.ANY)
SMEM = pl.BlockSpec(memory_space=pltpu.SMEM)


def params(limit=VMEM):
    return pltpu.CompilerParams(vmem_limit_bytes=limit)


def dot(a, b, contract=((1,), (0,))):
    return lax.dot_general(a, b, (contract, ((), ())), preferred_element_type=F32)


def iota(shape, axis):
    return lax.broadcasted_iota(jnp.int32, shape, axis)


def pack_kernel(pieces, replicas, cot_ref, gate_ref, route_ref, *out_refs):
    rows_own = cot_ref.shape[1] // replicas
    for out_ref, (start, width) in zip(out_refs, pieces):
        for q in range(replicas):
            at = q * rows_own + start
            out_ref[:, q * width : (q + 1) * width] = cot_ref[:, at : at + width]
    tokens = cot_ref.shape[0]
    line = iota((LANES, tokens), 0)
    half = LANES // 2
    gate = jnp.zeros((LANES, tokens), F32)
    hit = jnp.zeros((LANES, tokens), F32)
    for k in range(route_ref.shape[0]):
        named = route_ref[k : k + 1, :]
        gate = gate + jnp.where(named == line, gate_ref[k : k + 1, :].astype(F32), 0.0)
        hit = hit + jnp.where(named == line - half, 1.0, 0.0)
    earlier = (iota((tokens, tokens), 0) < iota((tokens, tokens), 1)).astype(F32).astype(BF16)
    rank = dot(hit.astype(BF16), earlier)
    table = jnp.where(line < half, gate, jnp.where(hit > 0, rank, NO_SLOT))
    first = out_refs[0]
    first[:, first.shape[1] - tokens :] = table.astype(BF16)


def pack(cotangent, gate_prob, routes, pieces, replicas):
    tokens = cotangent.shape[0]
    widths = [replicas * width for _, width in pieces]
    widths[0] += tokens
    return pl.pallas_call(
        functools.partial(pack_kernel, pieces, replicas),
        out_shape=[jax.ShapeDtypeStruct((tokens, width), BF16) for width in widths],
        compiler_params=params(),
        name="pack",
    )(cotangent, gate_prob.T, routes.T)


EDGE, MIDDLE = ((0, 1), (1, 0), (2, 3), (3, 2)), ((1, 2), (2, 1))
OUTWARD, INWARD = ((1, 0), (2, 3)), ((0, 1), (3, 2))


def along(value, pairs):
    return lax.ppermute(value, "expert", [(2 * a + x, 2 * b + x) for a, b in pairs for x in (0, 1)])


def across(value, rows):
    return lax.ppermute(value, "expert", [(2 * a + x, 2 * a + 1 - x) for a in rows for x in (0, 1)])


def fence(*values):
    return lax.optimization_barrier(values)


def line_slots():
    place = lax.axis_index("expert")
    line, side = place // 2, place % 2
    middle = (line == 1) | (line == 2)
    near = line ^ 1
    far = jnp.where(middle, 3 - line, 3 - near)
    last = far ^ 1
    lines = [line, near, far, far, last, last]
    valid = [True, True, middle, ~middle, middle, ~middle]
    same = [jnp.where(ok, 2 * at + side, -1) for at, ok in zip(lines, valid)]
    other = [jnp.where(ok, 2 * at + 1 - side, -1) for at, ok in zip(lines, valid)]
    return jnp.stack(same + other).astype(jnp.int32)


def load_parts(slots_ref, refs, tokens, dst_ref, sem):
    def each(action):
        for i, ref in enumerate(refs):

            @pl.when(slots_ref[i] >= 0)
            def _():
                at = pl.multiple_of(slots_ref[i] * tokens, tokens)
                action(pltpu.make_async_copy(ref, dst_ref.at[pl.ds(at, ref.shape[0]), :], sem.at[i]))

    each(lambda copy: copy.start())
    each(lambda copy: copy.wait())


def owner_of(j, groups):
    place = lax.axis_index("dp")
    chip, core = place // CORES, place % CORES
    owner_core = (1 - core) if j < groups else core
    return lax.rem(chip + j % groups + 1, groups) * CORES + owner_core


def hits(table, expert, experts_here, cap_rows):
    rank = table[experts_here + expert : experts_here + expert + 1, :]
    return iota((cap_rows, table.shape[1]), 0).astype(F32) == rank


def route_kernel(first, count, bands, width, groups, cap, slots_ref, *refs):
    parts, refs = refs[:count], refs[count:]
    if first:
        hidden_ref, refs = refs[0], refs[1:]
    else:
        weighted_ref, table_ref, refs = refs[0], refs[1], refs[2:]
    outs, refs = refs[: len(bands)], refs[len(bands) :]
    routed_out, refs = refs[0], refs[1:]
    if first:
        weighted_ref, table_ref, refs = refs[0], refs[1], refs[2:]
    rows, routed, part_sem, out_sem = refs
    expert = pl.program_id(0)
    experts_here, slots, columns = routed.shape
    sources, _, tokens = table_ref.shape
    cap_rows = slots // sources
    keep = pltpu.make_async_copy(routed, routed_out, out_sem)

    @pl.when(expert == 0)
    def _():
        load_parts(slots_ref, parts, tokens, rows, part_sem)
        if first:
            base = lax.axis_index("expert") * experts_here
            row, lane = iota((8, LANES), 0), iota((8, LANES), 1)
            wanted = base + jnp.where(row < experts_here, row, row - experts_here + LANES // 2)
            chosen = ((lane == wanted) & (row < 2 * experts_here)).astype(F32).astype(BF16)

        def fill(s, carry):
            at = pl.multiple_of(s * tokens, tokens)
            if first:
                table = dot(chosen, rows[pl.ds(at, tokens), columns : columns + tokens])
                table_ref[s] = table
            else:
                table = table_ref[s]
            picked = [hits(table, e, experts_here, cap_rows).astype(F32).astype(BF16) for e in range(experts_here)]
            got = dot(jnp.concatenate(picked, axis=0), rows[pl.ds(at, tokens), :columns]).astype(BF16)
            to = pl.multiple_of(s * cap_rows, cap_rows)
            for e in range(experts_here):
                routed[e, pl.ds(to, cap_rows), :] = got[e * cap_rows : (e + 1) * cap_rows, :]
            return carry

        lax.fori_loop(0, sources, fill, 0, unroll=sources <= 8)
        keep.start()

    if first:

        def weigh(s, carry):
            table = table_ref[s]
            line = iota(table.shape, 0)
            rank = jnp.sum(jnp.where(line == experts_here + expert, table, 0.0), axis=0, keepdims=True)
            prob = jnp.sum(jnp.where(line == expert, table, 0.0), axis=0, keepdims=True)
            hit = iota((cap, tokens), 0).astype(F32) == rank
            of_slot = jnp.sum(jnp.where(hit, prob, 0.0), axis=1, keepdims=True)
            scaled = of_slot * hidden_ref[0, s].astype(F32)
            if cap_rows > cap:
                scaled = jnp.concatenate([scaled, jnp.zeros((cap_rows - cap, scaled.shape[1]), F32)], axis=0)
            weighted_ref[0, pl.ds(pl.multiple_of(s * cap_rows, cap_rows), cap_rows), :] = scaled.astype(BF16)
            return carry

        lax.fori_loop(0, sources, weigh, 0, unroll=sources <= 8)

    grad_bands(routed.at[expert], weighted_ref, outs, bands, width, groups)

    @pl.when(expert == experts_here - 1)
    def _():
        keep.wait()


def grad_bands(routed, weighted_ref, outs, bands, width, groups):
    taken = []
    for band in bands:
        for j in band:
            at = pl.multiple_of(owner_of(j, groups) * width, LANES)
            taken.append(routed[:, pl.ds(at, width)])
    made = dot(jnp.concatenate(taken, axis=1), weighted_ref[0], ((0,), (0,))).astype(BF16)
    at = 0
    for out_ref, band in zip(outs, bands):
        out_ref[...] = made[at : at + len(band) * width, :]
        at += len(band) * width


def band_outputs(bands, width, experts_here, units):
    specs = [pl.BlockSpec((len(band) * width, units), lambda e: (0, e)) for band in bands]
    shapes = [jax.ShapeDtypeStruct((len(band) * width, experts_here * units), BF16) for band in bands]
    return specs, shapes


def route(parts, slots, width, bands, groups, tokens, hidden=None, weighted=None, table=None, cap=None):
    first = weighted is None
    if first:
        experts_here, sources, cap, units = hidden.shape
        cap_rows = -(-cap // 16) * 16
        slot_rows = sources * cap_rows
    else:
        experts_here, slot_rows, units = weighted.shape
        sources = table.shape[0]
    columns = parts[0].shape[1] - (tokens if first else 0)
    weighted_spec = pl.BlockSpec((1, slot_rows, units), lambda e: (e, 0, 0))
    table_spec = pl.BlockSpec((sources, 8, tokens), lambda e: (0, 0, 0))
    band_specs, band_shapes = band_outputs(bands, width, experts_here, units)
    routed_shape = jax.ShapeDtypeStruct((experts_here, slot_rows, columns), BF16)
    if first:
        operands = [hidden]
        in_specs = [pl.BlockSpec((1, sources, cap, units), lambda e: (e, 0, 0, 0))]
        more_specs = [weighted_spec, table_spec]
        more_shapes = [
            jax.ShapeDtypeStruct((experts_here, slot_rows, units), BF16),
            jax.ShapeDtypeStruct((sources, 8, tokens), F32),
        ]
    else:
        operands, in_specs, more_specs, more_shapes = [weighted, table], [weighted_spec, table_spec], [], []
    return pl.pallas_call(
        functools.partial(route_kernel, first, len(parts), bands, width, groups, cap),
        grid=(experts_here,),
        in_specs=[SMEM] + [ANY] * len(parts) + in_specs,
        out_specs=band_specs + [ANY] + more_specs,
        out_shape=band_shapes + [routed_shape] + more_shapes,
        scratch_shapes=[
            pltpu.VMEM((sources * tokens, parts[0].shape[1]), BF16),
            pltpu.VMEM((experts_here, slot_rows, columns), BF16),
            pltpu.SemaphoreType.DMA((len(parts),)),
            pltpu.SemaphoreType.DMA,
        ],
        compiler_params=params(),
        cost_estimate=pl.CostEstimate(
            flops=2 * slot_rows * experts_here * columns * (tokens + units),
            bytes_accessed=4 * slot_rows * experts_here * columns,
            transcendentals=0,
        ),
        name="route",
    )(slots, *parts, *operands)


def rest_kernel(bands, width, groups, routed_ref, weighted_ref, *outs):
    grad_bands(routed_ref.at[0], weighted_ref, outs, bands, width, groups)


def rest(routed, weighted, bands, width, groups):
    experts_here, slot_rows, columns = routed.shape
    units = weighted.shape[2]
    band_specs, band_shapes = band_outputs(bands, width, experts_here, units)
    return pl.pallas_call(
        functools.partial(rest_kernel, bands, width, groups),
        grid=(experts_here,),
        in_specs=[
            pl.BlockSpec((1, slot_rows, columns), lambda e: (e, 0, 0)),
            pl.BlockSpec((1, slot_rows, units), lambda e: (e, 0, 0)),
        ],
        out_specs=band_specs,
        out_shape=band_shapes,
        compiler_params=params(),
        cost_estimate=pl.CostEstimate(
            flops=slot_rows * experts_here * columns * units,
            bytes_accessed=4 * slot_rows * experts_here * columns,
            transcendentals=0,
        ),
        name="rest",
    )(routed, weighted)


def back_kernel(pieces, replicas, *refs):
    routed, refs = refs[: len(pieces)], refs[len(pieces) :]
    table_ref, weight_ref, hidden_ref, grad_ref, prob_ref, held = refs
    expert = pl.program_id(0)
    experts_here = pl.num_programs(0)
    _, sources, cap, units = hidden_ref.shape
    tokens = table_ref.shape[2]
    cap_rows = held.shape[0] // sources
    columns = []
    for q in range(replicas):
        for ref, (_, width) in zip(routed, pieces):
            columns.append(ref[0, :, q * width : (q + 1) * width])
    held[...] = dot(jnp.concatenate(columns, axis=1), weight_ref[0], ((1,), (1,)))

    def finish(s, carry):
        mine = held[pl.ds(pl.multiple_of(s * cap_rows, cap_rows), cap), :]
        table = table_ref[s]
        line = iota(table.shape, 0)
        rank = jnp.sum(jnp.where(line == experts_here + expert, table, 0.0), axis=0, keepdims=True)
        prob = jnp.sum(jnp.where(line == expert, table, 0.0), axis=0, keepdims=True)
        hit = iota((cap, tokens), 0).astype(F32) == rank
        of_slot = jnp.sum(jnp.where(hit, prob, 0.0), axis=1, keepdims=True)
        grad_ref[0, pl.ds(s, 1)] = (of_slot * mine).astype(BF16)[None]
        inner = jnp.sum(mine * hidden_ref[0, s].astype(F32), axis=1, keepdims=True)
        prob_ref[pl.ds(s, 1), pl.ds(expert, 1), :] = jnp.sum(jnp.where(hit, inner, 0.0), axis=0, keepdims=True)[None]
        return carry

    lax.fori_loop(0, sources, finish, 0, unroll=sources <= 8)


def back(routed, table, weight, hidden, pieces, replicas):
    experts_here, sources, cap, units = hidden.shape
    features = weight.shape[2]
    tokens = table.shape[2]
    slot_rows = routed[0].shape[1]
    return pl.pallas_call(
        functools.partial(back_kernel, pieces, replicas),
        grid=(experts_here,),
        in_specs=[pl.BlockSpec((1,) + part.shape[1:], lambda e: (e, 0, 0)) for part in routed]
        + [
            pl.BlockSpec(table.shape, lambda e: (0, 0, 0)),
            pl.BlockSpec((1, units, features), lambda e: (e, 0, 0)),
            pl.BlockSpec((1, sources, cap, units), lambda e: (e, 0, 0, 0)),
        ],
        out_specs=[
            pl.BlockSpec((1, sources, cap, units), lambda e: (e, 0, 0, 0)),
            pl.BlockSpec((sources, experts_here, tokens), lambda e: (0, 0, 0)),
        ],
        out_shape=[
            jax.ShapeDtypeStruct(hidden.shape, BF16),
            jax.ShapeDtypeStruct((sources, experts_here, tokens), F32),
        ],
        scratch_shapes=[pltpu.VMEM((slot_rows, units), F32)],
        compiler_params=params(),
        cost_estimate=pl.CostEstimate(
            flops=2 * experts_here * slot_rows * features * units,
            bytes_accessed=2 * (weight.size + 2 * hidden.size + experts_here * slot_rows * features),
            transcendentals=0,
        ),
        name="back",
    )(*routed, table, weight, hidden)


def rotate_kernel(count, experts_here, turn_ref, *refs):
    parts, out_ref = refs[:count], refs[-1]
    units = parts[0].shape[1] // experts_here
    total = parts[0][...].astype(F32)
    for ref in parts[1:]:
        total = total + ref[...].astype(F32)
    side = jnp.concatenate([total[:, e * units : (e + 1) * units] for e in range(experts_here)], axis=0)
    high = side.astype(BF16)
    low = (side - high.astype(F32)).astype(BF16)
    turn = turn_ref[0]
    turned = (dot(turn, high) + dot(turn, low)) * (1.0 / math.sqrt(BLOCK))
    out_ref[...] = turned.reshape(out_ref.shape)


def rotate(parts, turns, first_block, rows_out, experts_here, filled):
    rows, lines = parts[0].shape
    units = lines // experts_here
    extra = [] if filled is None else [filled]
    return pl.pallas_call(
        functools.partial(rotate_kernel, len(parts), experts_here),
        grid=(rows // BLOCK,),
        in_specs=[pl.BlockSpec((1,) + turns.shape[1:], lambda b: (first_block + b, 0, 0))]
        + [pl.BlockSpec((BLOCK, lines), lambda b: (b, 0)) for _ in parts]
        + [ANY] * len(extra),
        out_specs=pl.BlockSpec((BLOCK, experts_here, units), lambda b: (first_block + b, 0, 0)),
        out_shape=jax.ShapeDtypeStruct((rows_out, experts_here, units), F32),
        input_output_aliases={1 + len(parts): 0} if extra else {},
        compiler_params=params(),
        name="rotate",
    )(turns, *parts, *extra)


def turn_matrices(sign_seed, rows_own, experts_here):
    row = jnp.arange(BLOCK * experts_here, dtype=jnp.int32)
    anded = (row // experts_here)[:, None] & (row % BLOCK)[None, :]
    parity = sum(((anded >> shift) & 1) for shift in range(BLOCK.bit_length() - 1)) & 1
    same = (row % experts_here)[:, None] == (row // BLOCK)[None, :]
    matrix = jnp.where(same, 1 - 2 * parity, 0)
    own = lax.dynamic_slice_in_dim(2 * sign_seed - 1, lax.axis_index("dp") * rows_own, rows_own)
    signs = jnp.tile(own.reshape(-1, 1, BLOCK), (1, 1, experts_here))
    return (matrix[None] * signs).astype(BF16)


def shards(cotangent, gate_prob, routes, hidden, down_weight, sign_seed):
    tokens, features = cotangent.shape
    sources, replicas = lax.axis_size("expert"), lax.axis_size("dp")
    groups = replicas // CORES
    experts_here, units = down_weight.shape[0], down_weight.shape[1]
    rows_own = features // replicas
    saved = hidden[0]
    cap = saved.shape[2]
    width = rows_own // 2
    pieces = [(0, width), (width, width)]
    turns = turn_matrices(sign_seed, rows_own, experts_here)
    sent = pack(cotangent, gate_prob, routes, pieces, replicas)
    away_bands = [tuple(range(groups - 1)), tuple(range(groups, 2 * groups - 1))]
    here_bands = [(groups - 1,), (2 * groups - 1,)]

    def swap(value):
        return lax.ppermute(value, "dp", [(i, i ^ 1) for i in range(replicas)])

    def to_chips(value):
        moved = []
        for k in range(1, groups):
            pairs = [(i, (i // CORES + k) % groups * CORES + i % CORES) for i in range(replicas)]
            moved.append(lax.ppermute(value[(k - 1) * width : k * width], "dp", pairs))
        return moved

    def add(a, b):
        return (a.astype(F32) + b.astype(F32)).astype(BF16)

    def route_first(parts, slots):
        return route(parts, slots, width, away_bands + here_bands, groups, tokens, hidden=saved)

    if sources == 8:
        a, b = sent
        slots = line_slots()
        a_x0, a_s1, a_s2 = fence(across(a, range(4)), along(a, EDGE), along(a, MIDDLE))
        a_x1, a_s3, a_s4 = fence(across(a_s1, range(4)), along(a_s1, MIDDLE), along(a_s2, OUTWARD))
        a_x2, a_x4, a_s5 = fence(across(a_s2, (1, 2)), across(a_s4, (0, 3)), along(a_s3, OUTWARD))
        a_x3, a_x5, b, b_s1, b_s2 = fence(
            across(a_s3, (1, 2)), across(a_s5, (0, 3)), b, along(b, EDGE), along(b, MIDDLE)
        )
        a_parts = [a, a_s1, a_s2, a_s4, a_s3, a_s5, a_x0, a_x1, a_x2, a_x4, a_x3, a_x5]
        made = route_first(a_parts, slots)
        b_x0, b_s3, b_s4, *made = fence(across(b, range(4)), along(b_s1, MIDDLE), along(b_s2, OUTWARD), *made)
        away_send, away_keep, here_send, here_keep, routed_a, weighted, table = made
        away_got, here_got = swap(away_send), swap(here_send)
        away_sum = add(away_got, away_keep)
        b_x3, b_x4, b_w, b_s5, away_sum, here_got = fence(
            across(b_s3, (1, 2)), across(b_s4, (0, 3)), along(b_x0, INWARD), along(b_s3, OUTWARD), away_sum, here_got
        )
        final_a = [here_keep, here_got] + to_chips(away_sum)
        b_x2, b_x1, b_w5 = fence(across(b_s2, (1, 2)), across(b_s1, (0, 3)), along(b_x3, OUTWARD))
        b_parts = [b, b_s1, b_s2, b_s4, b_s3, b_s5, b_x0, b_x1, b_w, b_x2, b_x4, b_x3, b_w5]
        middle = (slots[2] >= 0)
        b_slots = jnp.concatenate(
            [
                slots[:7],
                jnp.where(middle, -1, slots[7:8]),
                jnp.where(middle, slots[7:8], -1),
                slots[8:],
            ]
        )
    else:
        a, b = [lax.all_gather(part, "expert", axis=0, tiled=True) for part in sent]
        slots = b_slots = jnp.zeros((1,), jnp.int32)
        a_parts, b_parts = [a], [b]
        made = route_first(a_parts, slots)
        away_send, away_keep, here_send, here_keep, routed_a, weighted, table = made
        final_a = [here_keep, swap(here_send)] + to_chips(add(swap(away_send), away_keep))

    away_send, away_keep, routed_b = route(
        b_parts, b_slots, width, away_bands, groups, tokens, weighted=weighted, table=table, cap=cap
    )
    arrived = to_chips(add(swap(away_send), away_keep))
    here_send, here_keep = rest(routed_b, weighted, here_bands, width, groups)
    final_b = [here_keep, swap(here_send)] + arrived

    grad_hidden, grad_slots = back([routed_a, routed_b], table, down_weight, saved, pieces, replicas)
    returned = lax.all_to_all(grad_slots, "expert", split_axis=0, concat_axis=0, tiled=True)
    of_token = returned.reshape(-1, 1, tokens)
    named = routes.T[None] == jnp.arange(of_token.shape[0], dtype=jnp.int32)[:, None, None]
    grad_prob = jnp.sum(jnp.where(named, of_token, 0.0), axis=0).T

    out = rotate(final_a, turns, 0, rows_own, experts_here, None)
    out = rotate(final_b, turns, width // BLOCK, rows_own, experts_here, out)
    return (grad_hidden[None], grad_prob, out)


def solution(mesh):
    in_specs = (
        P(("dp", "expert"), None),
        P(("dp", "expert"), None),
        P(("dp", "expert"), None),
        P("dp", "expert", None, None, None),
        P("expert", None, None),
        P(),
    )
    out_specs = (
        P("dp", "expert", None, None, None),
        P(("dp", "expert"), None),
        P("dp", "expert", None),
    )
    return jax.shard_map(shards, mesh=mesh, in_specs=in_specs, out_specs=out_specs, check_vma=False)
```

```python
import functools
import math

import jax
import jax.numpy as jnp
from jax import lax
from jax.experimental import pallas as pl
from jax.experimental.pallas import tpu as pltpu
from jax.sharding import PartitionSpec as P

BLOCK = 128
LANES = 128
CORES = 2
NO_SLOT = 512.0
VMEM = 56 * 1024 * 1024
F32 = jnp.float32
BF16 = jnp.bfloat16


ANY = pl.BlockSpec(memory_space=pl.ANY)
SMEM = pl.BlockSpec(memory_space=pltpu.SMEM)


def params(limit=VMEM):
    return pltpu.CompilerParams(vmem_limit_bytes=limit)


def dot(a, b, contract=((1,), (0,))):
    return lax.dot_general(a, b, (contract, ((), ())), preferred_element_type=F32)


def iota(shape, axis):
    return lax.broadcasted_iota(jnp.int32, shape, axis)


def pack_kernel(pieces, replicas, cot_ref, gate_ref, route_ref, *out_refs):
    rows_own = cot_ref.shape[1] // replicas
    for out_ref, (start, width) in zip(out_refs, pieces):
        for q in range(replicas):
            at = q * rows_own + start
            out_ref[:, q * width : (q + 1) * width] = cot_ref[:, at : at + width]
    tokens = cot_ref.shape[0]
    line = iota((LANES, tokens), 0)
    half = LANES // 2
    gate = jnp.zeros((LANES, tokens), F32)
    hit = jnp.zeros((LANES, tokens), F32)
    for k in range(route_ref.shape[0]):
        named = route_ref[k : k + 1, :]
        gate = gate + jnp.where(named == line, gate_ref[k : k + 1, :].astype(F32), 0.0)
        hit = hit + jnp.where(named == line - half, 1.0, 0.0)
    earlier = (iota((tokens, tokens), 0) < iota((tokens, tokens), 1)).astype(F32).astype(BF16)
    rank = dot(hit.astype(BF16), earlier)
    table = jnp.where(line < half, gate, jnp.where(hit > 0, rank, NO_SLOT))
    first = out_refs[0]
    first[:, first.shape[1] - tokens :] = table.astype(BF16)


def pack(cotangent, gate_prob, routes, pieces, replicas):
    tokens = cotangent.shape[0]
    widths = [replicas * width for _, width in pieces]
    widths[0] += tokens
    return pl.pallas_call(
        functools.partial(pack_kernel, pieces, replicas),
        out_shape=[jax.ShapeDtypeStruct((tokens, width), BF16) for width in widths],
        compiler_params=params(),
        name="pack",
    )(cotangent, gate_prob.T, routes.T)


LINES = 4


def along(value, by):
    pairs = [(line, (line + by) % LINES) for line in range(LINES)]
    return lax.ppermute(value, "expert", [(2 * a + x, 2 * b + x) for a, b in pairs for x in (0, 1)])


def across(value):
    return lax.ppermute(value, "expert", [(i, i ^ 1) for i in range(2 * LINES)])


def fence(*values):
    return lax.optimization_barrier(values)


def line_slots():
    place = lax.axis_index("expert")
    line, side = place // 2, place % 2
    lines = [line, (line + LINES - 1) % LINES, (line + 1) % LINES, (line + 2) % LINES]
    return jnp.stack([2 * at + side for at in lines] + [2 * at + 1 - side for at in lines]).astype(jnp.int32)


def load_parts(slots_ref, refs, tokens, dst_ref, sem):
    def each(action):
        for i, ref in enumerate(refs):

            @pl.when(slots_ref[i] >= 0)
            def _():
                at = pl.multiple_of(slots_ref[i] * tokens, tokens)
                action(pltpu.make_async_copy(ref, dst_ref.at[pl.ds(at, ref.shape[0]), :], sem.at[i]))

    each(lambda copy: copy.start())
    each(lambda copy: copy.wait())


def owner_of(j, groups):
    place = lax.axis_index("dp")
    chip, core = place // CORES, place % CORES
    owner_core = (1 - core) if j < groups else core
    return lax.rem(chip + j % groups + 1, groups) * CORES + owner_core


def hits(table, expert, experts_here, cap_rows):
    rank = table[experts_here + expert : experts_here + expert + 1, :]
    return iota((cap_rows, table.shape[1]), 0).astype(F32) == rank


def route_kernel(first, count, bands, width, groups, cap, slots_ref, *refs):
    parts, refs = refs[:count], refs[count:]
    if first:
        hidden_ref, refs = refs[0], refs[1:]
    else:
        weighted_ref, table_ref, refs = refs[0], refs[1], refs[2:]
    outs, refs = refs[: len(bands)], refs[len(bands) :]
    routed_out, refs = refs[0], refs[1:]
    if first:
        weighted_ref, table_ref, refs = refs[0], refs[1], refs[2:]
    rows, routed, part_sem, out_sem = refs
    expert = pl.program_id(0)
    experts_here, slots, columns = routed.shape
    sources, _, tokens = table_ref.shape
    cap_rows = slots // sources
    keep = pltpu.make_async_copy(routed, routed_out, out_sem)

    @pl.when(expert == 0)
    def _():
        load_parts(slots_ref, parts, tokens, rows, part_sem)
        if first:
            base = lax.axis_index("expert") * experts_here
            row, lane = iota((8, LANES), 0), iota((8, LANES), 1)
            wanted = base + jnp.where(row < experts_here, row, row - experts_here + LANES // 2)
            chosen = ((lane == wanted) & (row < 2 * experts_here)).astype(F32).astype(BF16)

        def fill(s, carry):
            at = pl.multiple_of(s * tokens, tokens)
            if first:
                table = dot(chosen, rows[pl.ds(at, tokens), columns : columns + tokens])
                table_ref[s] = table
            else:
                table = table_ref[s]
            picked = [hits(table, e, experts_here, cap_rows).astype(F32).astype(BF16) for e in range(experts_here)]
            got = dot(jnp.concatenate(picked, axis=0), rows[pl.ds(at, tokens), :columns]).astype(BF16)
            to = pl.multiple_of(s * cap_rows, cap_rows)
            for e in range(experts_here):
                routed[e, pl.ds(to, cap_rows), :] = got[e * cap_rows : (e + 1) * cap_rows, :]
            return carry

        lax.fori_loop(0, sources, fill, 0, unroll=sources <= 8)
        keep.start()

    if first:

        def weigh(s, carry):
            table = table_ref[s]
            line = iota(table.shape, 0)
            rank = jnp.sum(jnp.where(line == experts_here + expert, table, 0.0), axis=0, keepdims=True)
            prob = jnp.sum(jnp.where(line == expert, table, 0.0), axis=0, keepdims=True)
            hit = iota((cap, tokens), 0).astype(F32) == rank
            of_slot = jnp.sum(jnp.where(hit, prob, 0.0), axis=1, keepdims=True)
            scaled = of_slot * hidden_ref[0, s].astype(F32)
            if cap_rows > cap:
                scaled = jnp.concatenate([scaled, jnp.zeros((cap_rows - cap, scaled.shape[1]), F32)], axis=0)
            weighted_ref[0, pl.ds(pl.multiple_of(s * cap_rows, cap_rows), cap_rows), :] = scaled.astype(BF16)
            return carry

        lax.fori_loop(0, sources, weigh, 0, unroll=sources <= 8)

    grad_bands(routed.at[expert], weighted_ref, outs, bands, width, groups)

    @pl.when(expert == experts_here - 1)
    def _():
        keep.wait()


def grad_bands(routed, weighted_ref, outs, bands, width, groups):
    taken = []
    for band in bands:
        for j in band:
            at = pl.multiple_of(owner_of(j, groups) * width, LANES)
            taken.append(routed[:, pl.ds(at, width)])
    made = dot(jnp.concatenate(taken, axis=1), weighted_ref[0], ((0,), (0,))).astype(BF16)
    at = 0
    for out_ref, band in zip(outs, bands):
        out_ref[...] = made[at : at + len(band) * width, :]
        at += len(band) * width


def band_outputs(bands, width, experts_here, units):
    specs = [pl.BlockSpec((len(band) * width, units), lambda e: (0, e)) for band in bands]
    shapes = [jax.ShapeDtypeStruct((len(band) * width, experts_here * units), BF16) for band in bands]
    return specs, shapes


def route(parts, slots, width, bands, groups, tokens, hidden=None, weighted=None, table=None, cap=None):
    first = weighted is None
    if first:
        experts_here, sources, cap, units = hidden.shape
        cap_rows = -(-cap // 16) * 16
        slot_rows = sources * cap_rows
    else:
        experts_here, slot_rows, units = weighted.shape
        sources = table.shape[0]
    columns = parts[0].shape[1] - (tokens if first else 0)
    weighted_spec = pl.BlockSpec((1, slot_rows, units), lambda e: (e, 0, 0))
    table_spec = pl.BlockSpec((sources, 8, tokens), lambda e: (0, 0, 0))
    band_specs, band_shapes = band_outputs(bands, width, experts_here, units)
    routed_shape = jax.ShapeDtypeStruct((experts_here, slot_rows, columns), BF16)
    if first:
        operands = [hidden]
        in_specs = [pl.BlockSpec((1, sources, cap, units), lambda e: (e, 0, 0, 0))]
        more_specs = [weighted_spec, table_spec]
        more_shapes = [
            jax.ShapeDtypeStruct((experts_here, slot_rows, units), BF16),
            jax.ShapeDtypeStruct((sources, 8, tokens), F32),
        ]
    else:
        operands, in_specs, more_specs, more_shapes = [weighted, table], [weighted_spec, table_spec], [], []
    return pl.pallas_call(
        functools.partial(route_kernel, first, len(parts), bands, width, groups, cap),
        grid=(experts_here,),
        in_specs=[SMEM] + [ANY] * len(parts) + in_specs,
        out_specs=band_specs + [ANY] + more_specs,
        out_shape=band_shapes + [routed_shape] + more_shapes,
        scratch_shapes=[
            pltpu.VMEM((sources * tokens, parts[0].shape[1]), BF16),
            pltpu.VMEM((experts_here, slot_rows, columns), BF16),
            pltpu.SemaphoreType.DMA((len(parts),)),
            pltpu.SemaphoreType.DMA,
        ],
        compiler_params=params(),
        name="route",
    )(slots, *parts, *operands)


def back_kernel(replicas, last, *refs):
    routed_ref, weight_refs, refs = refs[0], refs[1 : 1 + replicas], refs[1 + replicas :]
    weight = jnp.concatenate([ref[0] for ref in weight_refs], axis=1)
    made = dot(routed_ref[0], weight, ((1,), (1,)))
    if not last:
        refs[0][0] = made.astype(BF16)
        return
    before_ref, table_ref, hidden_ref, grad_ref, prob_ref, held = refs
    expert = pl.program_id(0)
    experts_here = pl.num_programs(0)
    _, sources, cap, units = hidden_ref.shape
    tokens = table_ref.shape[2]
    cap_rows = held.shape[0] // sources
    held[...] = made + before_ref[0].astype(F32)

    def finish(s, carry):
        mine = held[pl.ds(pl.multiple_of(s * cap_rows, cap_rows), cap), :]
        table = table_ref[s]
        line = iota(table.shape, 0)
        rank = jnp.sum(jnp.where(line == experts_here + expert, table, 0.0), axis=0, keepdims=True)
        prob = jnp.sum(jnp.where(line == expert, table, 0.0), axis=0, keepdims=True)
        hit = iota((cap, tokens), 0).astype(F32) == rank
        of_slot = jnp.sum(jnp.where(hit, prob, 0.0), axis=1, keepdims=True)
        grad_ref[0, pl.ds(s, 1)] = (of_slot * mine).astype(BF16)[None]
        inner = jnp.sum(mine * hidden_ref[0, s].astype(F32), axis=1, keepdims=True)
        prob_ref[pl.ds(s, 1), pl.ds(expert, 1), :] = jnp.sum(jnp.where(hit, inner, 0.0), axis=0, keepdims=True)[None]
        return carry

    lax.fori_loop(0, sources, finish, 0, unroll=sources <= 8)


def back(routed, weight, start, replicas, before=None, table=None, hidden=None):
    experts_here, slot_rows, columns = routed.shape
    units, features = weight.shape[1:]
    width, rows_own = columns // replicas, features // replicas
    last = before is not None
    product = pl.BlockSpec((1, slot_rows, units), lambda e: (e, 0, 0))

    def share(q):
        return pl.BlockSpec((1, units, width), lambda e: (e, 0, (q * rows_own + start) // width))

    operands = [routed] + [weight] * replicas
    in_specs = [pl.BlockSpec((1, slot_rows, columns), lambda e: (e, 0, 0))] + [share(q) for q in range(replicas)]
    if last:
        sources, cap = hidden.shape[1:3]
        tokens = table.shape[2]
        saved = pl.BlockSpec((1, sources, cap, units), lambda e: (e, 0, 0, 0))
        operands += [before, table, hidden]
        in_specs += [product, pl.BlockSpec(table.shape, lambda e: (0, 0, 0)), saved]
        out_specs = [saved, pl.BlockSpec((sources, experts_here, tokens), lambda e: (0, 0, 0))]
        out_shape = [
            jax.ShapeDtypeStruct(hidden.shape, BF16),
            jax.ShapeDtypeStruct((sources, experts_here, tokens), F32),
        ]
    else:
        out_specs, out_shape = product, jax.ShapeDtypeStruct((experts_here, slot_rows, units), BF16)
    return pl.pallas_call(
        functools.partial(back_kernel, replicas, last),
        grid=(experts_here,),
        in_specs=in_specs,
        out_specs=out_specs,
        out_shape=out_shape,
        scratch_shapes=[pltpu.VMEM((slot_rows, units), F32)] if last else [],
        compiler_params=params(),
        name="back",
    )(*operands)


def rotate_kernel(count, experts_here, turn_ref, *refs):
    parts, out_ref = refs[:count], refs[-1]
    units = parts[0].shape[1] // experts_here
    total = parts[0][...].astype(F32)
    for ref in parts[1:]:
        total = total + ref[...].astype(F32)
    side = jnp.concatenate([total[:, e * units : (e + 1) * units] for e in range(experts_here)], axis=0)
    high = side.astype(BF16)
    low = (side - high.astype(F32)).astype(BF16)
    turn = turn_ref[0]
    turned = (dot(turn, high) + dot(turn, low)) * (1.0 / math.sqrt(BLOCK))
    out_ref[...] = turned.reshape(out_ref.shape)


def rotate(parts, turns, first_block, rows_out, experts_here, filled):
    rows, lines = parts[0].shape
    units = lines // experts_here
    extra = [] if filled is None else [filled]
    return pl.pallas_call(
        functools.partial(rotate_kernel, len(parts), experts_here),
        grid=(rows // BLOCK,),
        in_specs=[pl.BlockSpec((1,) + turns.shape[1:], lambda b: (first_block + b, 0, 0))]
        + [pl.BlockSpec((BLOCK, lines), lambda b: (b, 0)) for _ in parts]
        + [ANY] * len(extra),
        out_specs=pl.BlockSpec((BLOCK, experts_here, units), lambda b: (first_block + b, 0, 0)),
        out_shape=jax.ShapeDtypeStruct((rows_out, experts_here, units), F32),
        input_output_aliases={1 + len(parts): 0} if extra else {},
        compiler_params=params(),
        name="rotate",
    )(turns, *parts, *extra)


def turn_matrices(sign_seed, rows_own, experts_here):
    row = jnp.arange(BLOCK * experts_here, dtype=jnp.int32)
    anded = (row // experts_here)[:, None] & (row % BLOCK)[None, :]
    parity = sum(((anded >> shift) & 1) for shift in range(BLOCK.bit_length() - 1)) & 1
    same = (row % experts_here)[:, None] == (row // BLOCK)[None, :]
    matrix = jnp.where(same, 1 - 2 * parity, 0)
    own = lax.dynamic_slice_in_dim(2 * sign_seed - 1, lax.axis_index("dp") * rows_own, rows_own)
    signs = jnp.tile(own.reshape(-1, 1, BLOCK), (1, 1, experts_here))
    return (matrix[None] * signs).astype(BF16)


def shards(cotangent, gate_prob, routes, hidden, down_weight, sign_seed):
    tokens, features = cotangent.shape
    sources, replicas = lax.axis_size("expert"), lax.axis_size("dp")
    groups = replicas // CORES
    experts_here, units = down_weight.shape[0], down_weight.shape[1]
    rows_own = features // replicas
    saved = hidden[0]
    cap = saved.shape[2]
    width = rows_own // 2
    pieces = [(0, width), (width, width)]
    turns = turn_matrices(sign_seed, rows_own, experts_here)
    sent = pack(cotangent, gate_prob, routes, pieces, replicas)
    away_bands = [tuple(range(groups - 1)), tuple(range(groups, 2 * groups - 1))]
    here_bands = [(groups - 1,), (2 * groups - 1,)]

    def swap(value):
        return lax.ppermute(value, "dp", [(i, i ^ 1) for i in range(replicas)])

    def to_chips(value):
        moved = []
        for k in range(1, groups):
            pairs = [(i, (i // CORES + k) % groups * CORES + i % CORES) for i in range(replicas)]
            moved.append(lax.ppermute(value[(k - 1) * width : k * width], "dp", pairs))
        return moved

    def add(a, b):
        return (a.astype(F32) + b.astype(F32)).astype(BF16)

    bands = away_bands + here_bands

    def route_first(parts, slots):
        return route(parts, slots, width, bands, groups, tokens, hidden=saved)

    if sources == 2 * LINES:
        a, b = sent
        slots = line_slots()
        a_x, b_x, a_next, a_prev, a, b = fence(across(a), across(b), along(a, 1), along(a, -1), a, b)
        a_opp, a_xnext, a_xprev, b = fence(along(a, 2), across(a_next), across(a_prev), b)
        a_xopp, b_next, b_prev, b = fence(across(a_opp), along(b, 1), along(b, -1), b)
        b_opp, b_xnext, b_xprev = along(b, 2), across(b_next), across(b_prev)
        made = route_first([a, a_next, a_prev, a_opp, a_x, a_xnext, a_xprev, a_xopp], slots)
        b_opp, b_xnext, b_xprev, *made = fence(b_opp, b_xnext, b_xprev, *made)
        b_xopp = across(b_opp)
        away_send, away_keep, here_send, here_keep, routed_a, weighted, table = made
        away_sum = add(swap(away_send), away_keep)
        here_got = swap(here_send)
        a_arrived = to_chips(away_sum)
        product = back(routed_a, down_weight, 0, replicas)
        b_xopp, here_got, product = fence(b_xopp, here_got, product)
        b_parts = [b, b_next, b_prev, b_opp, b_x, b_xnext, b_xprev, b_xopp]
        b_slots = slots
    else:
        a, b = [lax.all_gather(part, "expert", axis=0, tiled=True) for part in sent]
        slots = b_slots = jnp.zeros((1,), jnp.int32)
        a_parts, b_parts = [a], [b]
        made = route_first(a_parts, slots)
        away_send, away_keep, here_send, here_keep, routed_a, weighted, table = made
        here_got = swap(here_send)
        a_arrived = to_chips(add(swap(away_send), away_keep))
        product = back(routed_a, down_weight, 0, replicas)

    made = route(b_parts, b_slots, width, bands, groups, tokens, weighted=weighted, table=table, cap=cap)
    made, a_arrived = fence(made, a_arrived)
    away_send, away_keep, here_send, here_keep_b, routed_b = made
    b_arrived = to_chips(add(swap(away_send), away_keep))
    here_got_b = swap(here_send)
    grad_hidden, grad_slots = back(routed_b, down_weight, width, replicas, product, table, saved)
    returned = lax.all_to_all(grad_slots, "expert", split_axis=0, concat_axis=0, tiled=True)
    out = rotate([here_keep, here_got] + a_arrived, turns, 0, rows_own, experts_here, None)
    out, returned, here_got_b, *b_arrived = fence(out, returned, here_got_b, *b_arrived)
    of_token = returned.reshape(-1, 1, tokens)
    named = routes.T[None] == jnp.arange(of_token.shape[0], dtype=jnp.int32)[:, None, None]
    grad_prob = jnp.sum(jnp.where(named, of_token, 0.0), axis=0).T
    out = rotate([here_keep_b, here_got_b] + b_arrived, turns, width // BLOCK, rows_own, experts_here, out)
    return (grad_hidden[None], grad_prob, out)


def solution(mesh):
    in_specs = (
        P(("dp", "expert"), None),
        P(("dp", "expert"), None),
        P(("dp", "expert"), None),
        P("dp", "expert", None, None, None),
        P("expert", None, None),
        P(),
    )
    out_specs = (
        P("dp", "expert", None, None, None),
        P(("dp", "expert"), None),
        P("dp", "expert", None),
    )
    return jax.shard_map(shards, mesh=mesh, in_specs=in_specs, out_specs=out_specs, check_vma=False)
```

```python
import functools
import math

import jax
import jax.numpy as jnp
from jax import lax
from jax.experimental import pallas as pl
from jax.experimental.pallas import tpu as pltpu
from jax.sharding import PartitionSpec as P

BLOCK = 128
LANES = 128
CORES = 2
NO_SLOT = 512.0
VMEM = 56 * 1024 * 1024
F32 = jnp.float32
BF16 = jnp.bfloat16


ANY = pl.BlockSpec(memory_space=pl.ANY)
HBM = pl.BlockSpec(memory_space=pltpu.HBM)
SMEM = pl.BlockSpec(memory_space=pltpu.SMEM)


def params(limit=VMEM):
    return pltpu.CompilerParams(vmem_limit_bytes=limit)


def dot(a, b, contract=((1,), (0,))):
    return lax.dot_general(a, b, (contract, ((), ())), preferred_element_type=F32)


def iota(shape, axis):
    return lax.broadcasted_iota(jnp.int32, shape, axis)


def pack_kernel(pieces, replicas, cot_ref, gate_ref, route_ref, *out_refs):
    rows_own = cot_ref.shape[1] // replicas
    for out_ref, (start, width) in zip(out_refs, pieces):
        for q in range(replicas):
            at = q * rows_own + start
            out_ref[:, q * width : (q + 1) * width] = cot_ref[:, at : at + width]
    tokens = cot_ref.shape[0]
    line = iota((LANES, tokens), 0)
    half = LANES // 2
    gate = jnp.zeros((LANES, tokens), F32)
    hit = jnp.zeros((LANES, tokens), F32)
    for k in range(route_ref.shape[0]):
        named = route_ref[k : k + 1, :]
        gate = gate + jnp.where(named == line, gate_ref[k : k + 1, :].astype(F32), 0.0)
        hit = hit + jnp.where(named == line - half, 1.0, 0.0)
    earlier = (iota((tokens, tokens), 0) < iota((tokens, tokens), 1)).astype(F32).astype(BF16)
    rank = dot(hit.astype(BF16), earlier)
    table = jnp.where(line < half, gate, jnp.where(hit > 0, rank, NO_SLOT))
    first = out_refs[0]
    first[:, first.shape[1] - tokens :] = table.astype(BF16)


def pack(cotangent, gate_prob, routes, pieces, replicas):
    tokens = cotangent.shape[0]
    widths = [replicas * width for _, width in pieces]
    widths[0] += tokens
    return pl.pallas_call(
        functools.partial(pack_kernel, pieces, replicas),
        out_shape=[jax.ShapeDtypeStruct((tokens, width), BF16) for width in widths],
        compiler_params=params(),
        name="pack",
    )(cotangent, gate_prob.T, routes.T)


LINES = 4


def along(value, by):
    pairs = [(line, (line + by) % LINES) for line in range(LINES)]
    return lax.ppermute(value, "expert", [(2 * a + x, 2 * b + x) for a, b in pairs for x in (0, 1)])


def across(value):
    return lax.ppermute(value, "expert", [(i, i ^ 1) for i in range(2 * LINES)])


def fence(*values):
    return lax.optimization_barrier(values)


def line_slots():
    place = lax.axis_index("expert")
    line, side = place // 2, place % 2
    before, behind, facing = (line + LINES - 1) % LINES, (line + 1) % LINES, (line + 2) % LINES
    near = [2 * line + side, 2 * line + 1 - side, 2 * before + side, 2 * behind + side]
    far = [2 * facing + side, 2 * before + 1 - side, 2 * behind + 1 - side]
    farthest = [2 * facing + 1 - side]
    return jnp.stack(near + far + farthest).astype(jnp.int32)


def hits(table, expert, experts_here, cap_rows):
    line = iota(table.shape, 0)
    rank = jnp.sum(jnp.where(line == experts_here + expert, table, 0.0), axis=0, keepdims=True)
    prob = jnp.sum(jnp.where(line == expert, table, 0.0), axis=0, keepdims=True)
    return iota((cap_rows, table.shape[1]), 0).astype(F32) == rank, prob


def fill_slots(rows, routed, tables, sources):
    experts_here, slot_rows, columns = routed.shape
    cap_rows = slot_rows // sources
    tokens = rows.shape[0] // sources

    def fill(first, table_ref, s):
        table = table_ref[s]
        picked = [hits(table, e, experts_here, cap_rows)[0].astype(F32).astype(BF16) for e in range(experts_here)]
        at = pl.multiple_of((first + s) * tokens, tokens)
        got = dot(jnp.concatenate(picked, axis=0), rows[pl.ds(at, tokens), :columns]).astype(BF16)
        to = pl.multiple_of((first + s) * cap_rows, cap_rows)
        for e in range(experts_here):
            routed[e, pl.ds(to, cap_rows), :] = got[e * cap_rows : (e + 1) * cap_rows, :]

    first = 0
    for table_ref in tables:
        each(table_ref.shape[0], functools.partial(fill, first, table_ref))
        first += table_ref.shape[0]


def each(count, body):
    def step(s, carry):
        body(s)
        return carry

    lax.fori_loop(0, count, step, 0, unroll=count <= 8)


def part_copies(parts, rows, sem):
    size = rows.shape[0] // len(parts)
    return [
        pltpu.make_async_copy(part, rows.at[pl.ds(i * size, size), :], sem.at[i]) for i, part in enumerate(parts)
    ]


def whole(part):
    return pl.BlockSpec((1,) + part.shape[1:], lambda e, *_: (e, 0, 0))


def weight_share(weight, columns, replicas, start):
    units, features = weight.shape[1:]
    width, rows_own = columns // replicas, features // replicas

    def share(q):
        return pl.BlockSpec((1, units, width), lambda e: (e, 0, (q * rows_own + start) // width))

    return [share(q) for q in range(replicas)]


def joined(refs):
    return jnp.concatenate([ref[0] for ref in refs], axis=1)


def visit_kernel(parts_here, shares, begin, slots_ref, *refs):
    parts, refs = refs[:parts_here], refs[parts_here:]
    weight_refs, refs = refs[:shares], refs[shares:]
    hidden_hbm, routed_ref, weighted_ref, table_ref = refs[:4]
    product_ref = refs[4] if shares else None
    rows, routed, saved, part_sem, saved_sem = refs[-5:]
    expert = pl.program_id(0)
    experts_here, slot_rows, columns = routed.shape
    _, count, cap, units = saved.shape
    tokens = table_ref.shape[2]
    cap_rows = slot_rows // count

    def saved_copies(s):
        return pltpu.make_async_copy(hidden_hbm.at[:, slots_ref[begin + s]], saved.at[:, s], saved_sem.at[s])

    @pl.when(expert == 0)
    def _():
        for copy in part_copies(parts, rows, part_sem):
            copy.start()
        each(count, lambda s: saved_copies(s).start())
        for copy in part_copies(parts, rows, part_sem):
            copy.wait()
        base = lax.axis_index("expert") * experts_here
        row, lane = iota((8, LANES), 0), iota((8, LANES), 1)
        wanted = base + jnp.where(row < experts_here, row, row - experts_here + LANES // 2)
        chosen = ((lane == wanted) & (row < 2 * experts_here)).astype(F32).astype(BF16)

        def look_up(s):
            at = pl.multiple_of(s * tokens, tokens)
            table_ref[s] = dot(chosen, rows[pl.ds(at, tokens), columns : columns + tokens])

        each(count, look_up)
        fill_slots(rows, routed, [table_ref], count)
        each(count, lambda s: saved_copies(s).wait())

    routed_ref[0] = routed[expert]
    if shares:
        product_ref[0] = dot(routed[expert], joined(weight_refs), ((1,), (1,))).astype(BF16)

    def weigh(s):
        hit, prob = hits(table_ref[s], expert, experts_here, cap)
        of_slot = jnp.sum(jnp.where(hit, prob, 0.0), axis=1, keepdims=True)
        scaled = of_slot * saved[expert, s].astype(F32)
        if cap_rows > cap:
            scaled = jnp.concatenate([scaled, jnp.zeros((cap_rows - cap, units), F32)], axis=0)
        weighted_ref[0, pl.ds(pl.multiple_of(s * cap_rows, cap_rows), cap_rows), :] = scaled.astype(BF16)

    each(count, weigh)


def visit(parts, slots, begin, weight, hidden, replicas, tokens, with_product=True):
    experts_here, _, cap, units = hidden.shape
    cap_rows = -(-cap // 16) * 16
    count = sum(part.shape[0] for part in parts) // tokens
    slot_rows = count * cap_rows
    columns = parts[0].shape[1] - tokens
    shares = weight_share(weight, columns, replicas, 0) if with_product else []
    product = jax.ShapeDtypeStruct((experts_here, slot_rows, units), BF16)
    routed = jax.ShapeDtypeStruct((experts_here, slot_rows, columns), BF16)
    table = jax.ShapeDtypeStruct((count, 8, tokens), F32)
    return pl.pallas_call(
        functools.partial(visit_kernel, len(parts), len(shares), begin),
        grid=(experts_here,),
        in_specs=[SMEM] + [HBM] * len(parts) + shares + [HBM],
        out_specs=[whole(routed), whole(product), pl.BlockSpec(table.shape, lambda e: (0, 0, 0))]
        + [whole(product)] * with_product,
        out_shape=[routed, product, table] + [product] * with_product,
        scratch_shapes=[
            pltpu.VMEM((count * tokens, parts[0].shape[1]), BF16),
            pltpu.VMEM((experts_here, slot_rows, columns), BF16),
            pltpu.VMEM((experts_here, count, cap, units), BF16),
            pltpu.SemaphoreType.DMA((len(parts),)),
            pltpu.SemaphoreType.DMA((count,)),
        ],
        compiler_params=params(),
        name="visit",
    )(slots, *parts, *[weight] * len(shares), hidden)


def owners(replicas):
    place = lax.axis_index("dp")
    groups = replicas // CORES
    chip, core = place // CORES, place % CORES
    away = [(chip + j + 1) % groups * CORES for j in range(groups)]
    return jnp.stack([at + 1 - core for at in away] + [at + core for at in away]).astype(jnp.int32)


def store_bands(taken, weighted_refs, outs):
    weighted = jnp.concatenate([ref[0] for ref in weighted_refs], axis=0)
    made = dot(taken, weighted, ((0,), (0,))).astype(BF16)
    at = 0
    for out_ref in outs:
        out_ref[...] = made[at : at + out_ref.shape[0], :]
        at += out_ref.shape[0]


def band_outputs(bands, width, experts_here, units):
    rows = [len(band) * width for band in bands]
    rows = [rows[0] // 2, rows[0] // 2] + rows[1:]
    specs = [pl.BlockSpec((size, units), lambda e, *_: (0, e)) for size in rows]
    shapes = [jax.ShapeDtypeStruct((size, experts_here * units), BF16) for size in rows]
    return specs, shapes


def bands_kernel(total, groups_here, weighted_here, owners_ref, *refs):
    taken = [
        jnp.concatenate([ref[0] for ref in refs[j * groups_here : (j + 1) * groups_here]], axis=0)
        for j in range(total)
    ]
    refs = refs[total * groups_here :]
    store_bands(jnp.concatenate(taken, axis=1), refs[:weighted_here], refs[weighted_here:])


def grad_bands(routed, weighted, owned, bands):
    experts_here, _, units = weighted[0].shape
    width = routed[0].shape[2] // owned.shape[0]
    wanted = [j for band in bands for j in band]
    out_specs, out_shape = band_outputs(bands, width, experts_here, units)

    def share(part, j):
        return pl.BlockSpec((1, part.shape[1], width), lambda e, owned: (e, 0, owned[j]))

    return pl.pallas_call(
        functools.partial(bands_kernel, len(wanted), len(routed), len(weighted)),
        grid_spec=pltpu.PrefetchScalarGridSpec(
            num_scalar_prefetch=1,
            grid=(experts_here,),
            in_specs=[share(part, j) for j in wanted for part in routed] + [whole(part) for part in weighted],
            out_specs=out_specs,
        ),
        out_shape=out_shape,
        compiler_params=params(),
        name="bands",
    )(owned, *[part for _ in wanted for part in routed], *weighted)


def route_kernel(parts_here, groups_here, wanted, width, owners_ref, *refs):
    parts, refs = refs[:parts_here], refs[parts_here:]
    tables, refs = refs[:groups_here], refs[groups_here:]
    weighted, refs = refs[:groups_here], refs[groups_here:]
    outs, (routed_hbm, rows, routed, part_sem, out_sem) = refs[:-5], refs[-5:]
    expert = pl.program_id(0)
    keep = pltpu.make_async_copy(routed, routed_hbm, out_sem)

    @pl.when(expert == 0)
    def _():
        for copy in part_copies(parts, rows, part_sem):
            copy.start()
        for copy in part_copies(parts, rows, part_sem):
            copy.wait()
        fill_slots(rows, routed, tables, sum(table.shape[0] for table in tables))
        keep.start()

    taken = [routed[expert, :, pl.ds(pl.multiple_of(owners_ref[j] * width, LANES), width)] for j in wanted]
    store_bands(jnp.concatenate(taken, axis=1), weighted, outs)

    @pl.when(expert == pl.num_programs(0) - 1)
    def _():
        keep.wait()


def route(parts, tables, weighted, owned, bands):
    experts_here, _, units = weighted[0].shape
    slot_rows = sum(part.shape[1] for part in weighted)
    token_rows, tokens = sum(part.shape[0] for part in parts), tables[0].shape[2]
    columns = parts[0].shape[1]
    width = columns // owned.shape[0]
    out_specs, out_shape = band_outputs(bands, width, experts_here, units)
    wanted = [j for band in bands for j in band]
    return pl.pallas_call(
        functools.partial(route_kernel, len(parts), len(tables), wanted, width),
        grid=(experts_here,),
        in_specs=[SMEM]
        + [HBM] * len(parts)
        + [pl.BlockSpec(table.shape, lambda e: (0, 0, 0)) for table in tables]
        + [whole(part) for part in weighted],
        out_specs=out_specs + [HBM],
        out_shape=out_shape + [jax.ShapeDtypeStruct((experts_here, slot_rows, columns), BF16)],
        scratch_shapes=[
            pltpu.VMEM((token_rows, columns), BF16),
            pltpu.VMEM((experts_here, slot_rows, columns), BF16),
            pltpu.SemaphoreType.DMA((len(parts),)),
            pltpu.SemaphoreType.DMA,
        ],
        compiler_params=params(),
        cost_estimate=pl.CostEstimate(
            flops=2 * experts_here * slot_rows * columns * (units + tokens), bytes_accessed=10_000_000, transcendentals=0
        ),
        name="route",
    )(owned, *parts, *tables, *weighted)


def back_kernel(shares, seen_here, late_here, groups_here, slots_ref, routed_ref, *refs):
    last_weights, refs = refs[:shares], refs[shares:]
    first_weights, refs = refs[: shares * late_here], refs[shares * late_here :]
    late, refs = refs[:late_here], refs[late_here:]
    seen, refs = refs[:seen_here], refs[seen_here:]
    tables, refs = refs[:groups_here], refs[groups_here:]
    hidden_ref, grad_ref, prob_ref, held = refs
    expert = pl.program_id(0)
    experts_here = pl.num_programs(0)
    _, sources, cap, units = hidden_ref.shape
    cap_rows = held.shape[0] // sources
    before = [ref[0].astype(F32) for ref in seen]
    before += [dot(ref[0], joined(first_weights), ((1,), (1,))) for ref in late]
    held[...] = dot(routed_ref[0], joined(last_weights), ((1,), (1,))) + jnp.concatenate(before, axis=0)

    def finish(first, table_ref, s):
        at = first + s
        source = slots_ref[at]
        mine = held[pl.ds(pl.multiple_of(at * cap_rows, cap_rows), cap), :]
        hit, prob = hits(table_ref[s], expert, experts_here, cap)
        of_slot = jnp.sum(jnp.where(hit, prob, 0.0), axis=1, keepdims=True)
        grad_ref[0, pl.ds(source, 1)] = (of_slot * mine).astype(BF16)[None]
        inner = jnp.sum(mine * hidden_ref[0, source].astype(F32), axis=1, keepdims=True)
        gate = jnp.sum(jnp.where(hit, inner, 0.0), axis=0, keepdims=True)
        prob_ref[pl.ds(source, 1), pl.ds(expert, 1), :] = gate[None]

    first = 0
    for table_ref in tables:
        each(table_ref.shape[0], functools.partial(finish, first, table_ref))
        first += table_ref.shape[0]


def back(routed, slots, weight, hidden, start, replicas, seen, late, tables):
    experts_here, sources, cap, units = hidden.shape
    columns = routed.shape[2]
    tokens = tables[0].shape[2]
    saved = pl.BlockSpec((1, sources, cap, units), lambda e: (e, 0, 0, 0))
    return pl.pallas_call(
        functools.partial(back_kernel, replicas, len(seen), len(late), len(tables)),
        grid=(experts_here,),
        in_specs=[SMEM, whole(routed)]
        + weight_share(weight, columns, replicas, start)
        + weight_share(weight, columns, replicas, 0) * len(late)
        + [whole(part) for part in late]
        + [whole(part) for part in seen]
        + [pl.BlockSpec(table.shape, lambda e: (0, 0, 0)) for table in tables]
        + [saved],
        out_specs=[saved, pl.BlockSpec((sources, experts_here, tokens), lambda e: (0, 0, 0))],
        out_shape=[
            jax.ShapeDtypeStruct(hidden.shape, BF16),
            jax.ShapeDtypeStruct((sources, experts_here, tokens), F32),
        ],
        scratch_shapes=[pltpu.VMEM((routed.shape[1], units), F32)],
        compiler_params=params(),
        name="back",
    )(slots, routed, *[weight] * (replicas * (1 + len(late))), *late, *seen, *tables, hidden)


def rotate_kernel(count, experts_here, turn_ref, *refs):
    parts, out_ref = refs[:count], refs[-1]
    units = parts[0].shape[1] // experts_here
    total = parts[0][...].astype(F32)
    for ref in parts[1:]:
        total = total + ref[...].astype(F32)
    side = jnp.concatenate([total[:, e * units : (e + 1) * units] for e in range(experts_here)], axis=0)
    high = side.astype(BF16)
    low = (side - high.astype(F32)).astype(BF16)
    turn = turn_ref[0]
    turned = (dot(turn, high) + dot(turn, low)) * (1.0 / math.sqrt(BLOCK))
    out_ref[...] = turned.reshape(out_ref.shape)


def rotate(parts, turns, first_block, rows_out, experts_here, filled):
    rows, lines = parts[0].shape
    units = lines // experts_here
    extra = [] if filled is None else [filled]
    return pl.pallas_call(
        functools.partial(rotate_kernel, len(parts), experts_here),
        grid=(rows // BLOCK,),
        in_specs=[pl.BlockSpec((1,) + turns.shape[1:], lambda b: (first_block + b, 0, 0))]
        + [pl.BlockSpec((BLOCK, lines), lambda b: (b, 0)) for _ in parts]
        + [ANY] * len(extra),
        out_specs=pl.BlockSpec((BLOCK, experts_here, units), lambda b: (first_block + b, 0, 0)),
        out_shape=jax.ShapeDtypeStruct((rows_out, experts_here, units), F32),
        input_output_aliases={1 + len(parts): 0} if extra else {},
        compiler_params=params(),
        name="rotate",
    )(turns, *parts, *extra)


def turn_matrices(sign_seed, rows_own, experts_here):
    row = jnp.arange(BLOCK * experts_here, dtype=jnp.int32)
    anded = (row // experts_here)[:, None] & (row % BLOCK)[None, :]
    parity = sum(((anded >> shift) & 1) for shift in range(BLOCK.bit_length() - 1)) & 1
    same = (row % experts_here)[:, None] == (row // BLOCK)[None, :]
    matrix = jnp.where(same, 1 - 2 * parity, 0)
    own = lax.dynamic_slice_in_dim(2 * sign_seed - 1, lax.axis_index("dp") * rows_own, rows_own)
    signs = jnp.tile(own.reshape(-1, 1, BLOCK), (1, 1, experts_here))
    return (matrix[None] * signs).astype(BF16)


def shards(cotangent, gate_prob, routes, hidden, down_weight, sign_seed):
    tokens, features = cotangent.shape
    sources, replicas = lax.axis_size("expert"), lax.axis_size("dp")
    groups = replicas // CORES
    experts_here, units = down_weight.shape[0], down_weight.shape[1]
    rows_own = features // replicas
    saved = hidden[0]
    cap = saved.shape[2]
    width = rows_own // 2
    pieces = [(0, width), (width, width)]
    turns = turn_matrices(sign_seed, rows_own, experts_here)
    sent = pack(cotangent, gate_prob, routes, pieces, replicas)
    owned = owners(replicas)
    away_bands = [tuple(range(groups - 1)), tuple(range(groups, 2 * groups - 1))]
    here_bands = [(groups - 1,), (2 * groups - 1,)]

    def swap(value):
        return lax.ppermute(value, "dp", [(i, i ^ 1) for i in range(replicas)])

    def to_chips(value):
        moved = []
        for k in range(1, groups):
            pairs = [(i, (i // CORES + k) % groups * CORES + i % CORES) for i in range(replicas)]
            moved.append(lax.ppermute(value[(k - 1) * width : k * width], "dp", pairs))
        return moved

    def add_swapped(halves, kept):
        got = jnp.concatenate([swap(half) for half in halves], axis=0)
        return (got.astype(F32) + kept.astype(F32)).astype(BF16)

    def visit_first(parts, begin, with_product=True):
        return visit(parts, slots, begin, down_weight, saved, replicas, tokens, with_product)

    def bands_first(visits, bands):
        return grad_bands([made[0] for made in visits], [made[1] for made in visits], owned, bands)

    a, b = sent
    if sources == 2 * LINES:
        a_x, b_x, a_next, a_prev, a, b, turns, owned, slots = fence(
            across(a), across(b), along(a, 1), along(a, -1), a, b, turns, owned, line_slots()
        )
        a_opp, a_xnext, a_xprev = along(a, 2), across(a_next), across(a_prev)
        a_near = visit_first([a, a_x, a_next, a_prev], 0)
        a_opp, a_xnext, a_xprev, a_near, b = fence(a_opp, a_xnext, a_xprev, a_near, b)
        a_xopp, b_next, b_prev = across(a_opp), along(b, 1), along(b, -1)
        a_far = visit_first([a_opp, a_xnext, a_xprev], 4)
        a_xopp, b_next, b_prev, a_far, b = fence(a_xopp, b_next, b_prev, a_far, b)
        b_opp, b_xnext, b_xprev = along(b, 2), across(b_next), across(b_prev)
        a_made = [a_near, a_far, visit_first([a_xopp], 7, with_product=False)]
        made = bands_first(a_made, away_bands + here_bands)
        b_opp, b_xnext, b_xprev, made = fence(b_opp, b_xnext, b_xprev, made)
        *away_send, away_keep, here_send, here_keep = made
        b_xopp = across(b_opp)
        a_arrived = to_chips(add_swapped(away_send, away_keep))
        b_xopp, here_send = fence(b_xopp, here_send)
        b_parts = [b, b_x, b_next, b_prev, b_opp, b_xnext, b_xprev, b_xopp]
        seen, late = [a_near[3], a_far[3]], [a_made[2][0]]
    else:
        a, b = [lax.all_gather(part, "expert", axis=0, tiled=True) for part in sent]
        slots = jnp.arange(sources, dtype=jnp.int32)
        a_made = [visit_first([a], 0)]
        *away_send, away_keep, here_send, here_keep = bands_first(a_made, away_bands + here_bands)
        a_arrived = to_chips(add_swapped(away_send, away_keep))
        b_parts = [b]
        seen, late = [a_made[0][3]], []

    weighted = [made[1] for made in a_made]
    tables = [made[2] for made in a_made]
    made = route(b_parts, tables, weighted, owned, away_bands + here_bands)
    *away_send, away_keep, here_send_b, here_keep_b, routed_b = made
    away_keep, a_arrived = fence(away_keep, a_arrived)
    b_arrived = to_chips(add_swapped(away_send, away_keep))
    here_got, here_got_b = swap(here_send), swap(here_send_b)
    grad_hidden, grad_slots = back(routed_b, slots, down_weight, saved, width, replicas, seen, late, tables)
    returned = lax.all_to_all(grad_slots, "expert", split_axis=0, concat_axis=0, tiled=True)
    out = rotate([here_keep, here_got] + a_arrived, turns, 0, rows_own, experts_here, None)
    out, returned, *b_arrived = fence(out, returned, *b_arrived)
    of_token = returned.reshape(-1, 1, tokens)
    named = routes.T[None] == jnp.arange(of_token.shape[0], dtype=jnp.int32)[:, None, None]
    grad_prob = jnp.sum(jnp.where(named, of_token, 0.0), axis=0).T
    out = rotate([here_keep_b, here_got_b] + b_arrived, turns, width // BLOCK, rows_own, experts_here, out)
    return (grad_hidden[None], grad_prob, out)


def solution(mesh):
    in_specs = (
        P(("dp", "expert"), None),
        P(("dp", "expert"), None),
        P(("dp", "expert"), None),
        P("dp", "expert", None, None, None),
        P("expert", None, None),
        P(),
    )
    out_specs = (
        P("dp", "expert", None, None, None),
        P(("dp", "expert"), None),
        P("dp", "expert", None),
    )
    return jax.shard_map(shards, mesh=mesh, in_specs=in_specs, out_specs=out_specs, check_vma=False)
```

```python
import functools
import math

import jax
import jax.numpy as jnp
from jax import lax
from jax.experimental import pallas as pl
from jax.experimental.pallas import tpu as pltpu
from jax.sharding import PartitionSpec as P

BLOCK = 128
LANES = 128
CORES = 2
NO_SLOT = 512.0
VMEM = 56 * 1024 * 1024
F32 = jnp.float32
BF16 = jnp.bfloat16


ANY = pl.BlockSpec(memory_space=pl.ANY)
HBM = pl.BlockSpec(memory_space=pltpu.HBM)
SMEM = pl.BlockSpec(memory_space=pltpu.SMEM)


def params(limit=VMEM):
    return pltpu.CompilerParams(vmem_limit_bytes=limit)


def dot(a, b, contract=((1,), (0,))):
    return lax.dot_general(a, b, (contract, ((), ())), preferred_element_type=F32)


def iota(shape, axis):
    return lax.broadcasted_iota(jnp.int32, shape, axis)


def pack_kernel(pieces, replicas, cot_ref, gate_ref, route_ref, *out_refs):
    rows_own = cot_ref.shape[1] // replicas
    for out_ref, (start, width) in zip(out_refs, pieces):
        for q in range(replicas):
            at = q * rows_own + start
            out_ref[:, q * width : (q + 1) * width] = cot_ref[:, at : at + width]
    tokens = cot_ref.shape[0]
    line = iota((LANES, tokens), 0)
    half = LANES // 2
    gate = jnp.zeros((LANES, tokens), F32)
    hit = jnp.zeros((LANES, tokens), F32)
    for k in range(route_ref.shape[0]):
        named = route_ref[k : k + 1, :]
        gate = gate + jnp.where(named == line, gate_ref[k : k + 1, :].astype(F32), 0.0)
        hit = hit + jnp.where(named == line - half, 1.0, 0.0)
    earlier = (iota((tokens, tokens), 0) < iota((tokens, tokens), 1)).astype(F32).astype(BF16)
    rank = dot(hit.astype(BF16), earlier)
    table = jnp.where(line < half, gate, jnp.where(hit > 0, rank, NO_SLOT))
    first = out_refs[0]
    first[:, first.shape[1] - tokens :] = table.astype(BF16)


def pack(cotangent, gate_prob, routes, pieces, replicas):
    tokens = cotangent.shape[0]
    widths = [replicas * width for _, width in pieces]
    widths[0] += tokens
    return pl.pallas_call(
        functools.partial(pack_kernel, pieces, replicas),
        out_shape=[jax.ShapeDtypeStruct((tokens, width), BF16) for width in widths],
        compiler_params=params(),
        name="pack",
    )(cotangent, gate_prob.T, routes.T)


LINES = 4


def along(value, by):
    pairs = [(line, (line + by) % LINES) for line in range(LINES)]
    return lax.ppermute(value, "expert", [(2 * a + x, 2 * b + x) for a, b in pairs for x in (0, 1)])


def across(value):
    return lax.ppermute(value, "expert", [(i, i ^ 1) for i in range(2 * LINES)])


def fence(*values):
    return lax.optimization_barrier(values)


def line_slots():
    place = lax.axis_index("expert")
    line, side = place // 2, place % 2
    before, behind, facing = (line + LINES - 1) % LINES, (line + 1) % LINES, (line + 2) % LINES
    near = [2 * line + side, 2 * line + 1 - side, 2 * before + side, 2 * behind + side]
    far = [2 * facing + side, 2 * before + 1 - side, 2 * behind + 1 - side]
    farthest = [2 * facing + 1 - side]
    return jnp.stack(near + far + farthest).astype(jnp.int32)


def hits(table, expert, experts_here, cap_rows):
    line = iota(table.shape, 0)
    rank = jnp.sum(jnp.where(line == experts_here + expert, table, 0.0), axis=0, keepdims=True)
    prob = jnp.sum(jnp.where(line == expert, table, 0.0), axis=0, keepdims=True)
    return iota((cap_rows, table.shape[1]), 0).astype(F32) == rank, prob


def fill_slots(rows, routed, tables, sources):
    experts_here, slot_rows, columns = routed.shape
    cap_rows = slot_rows // sources
    tokens = rows.shape[0] // sources

    def fill(first, table_ref, s):
        table = table_ref[s]
        picked = [hits(table, e, experts_here, cap_rows)[0].astype(F32).astype(BF16) for e in range(experts_here)]
        at = pl.multiple_of((first + s) * tokens, tokens)
        got = dot(jnp.concatenate(picked, axis=0), rows[pl.ds(at, tokens), :columns]).astype(BF16)
        to = pl.multiple_of((first + s) * cap_rows, cap_rows)
        for e in range(experts_here):
            routed[e, pl.ds(to, cap_rows), :] = got[e * cap_rows : (e + 1) * cap_rows, :]

    first = 0
    for table_ref in tables:
        each(table_ref.shape[0], functools.partial(fill, first, table_ref))
        first += table_ref.shape[0]


def each(count, body):
    def step(s, carry):
        body(s)
        return carry

    lax.fori_loop(0, count, step, 0, unroll=count <= 8)


def part_copies(parts, rows, sem):
    size = rows.shape[0] // len(parts)
    return [
        pltpu.make_async_copy(part, rows.at[pl.ds(i * size, size), :], sem.at[i]) for i, part in enumerate(parts)
    ]


def whole(part):
    return pl.BlockSpec((1,) + part.shape[1:], lambda e, *_: (e, 0, 0))


def weight_share(weight, columns, replicas, start):
    units, features = weight.shape[1:]
    width, rows_own = columns // replicas, features // replicas

    def share(q):
        return pl.BlockSpec((1, units, width), lambda e: (e, 0, (q * rows_own + start) // width))

    return [share(q) for q in range(replicas)]


def joined(refs):
    return jnp.concatenate([ref[0] for ref in refs], axis=1)


def visit_kernel(parts_here, shares, begin, slots_ref, *refs):
    parts, refs = refs[:parts_here], refs[parts_here:]
    weight_refs, refs = refs[:shares], refs[shares:]
    hidden_hbm, routed_ref, weighted_ref, table_ref = refs[:4]
    product_ref = refs[4] if shares else None
    rows, routed, saved, part_sem, saved_sem = refs[-5:]
    expert = pl.program_id(0)
    experts_here, slot_rows, columns = routed.shape
    _, count, cap, units = saved.shape
    tokens = table_ref.shape[2]
    cap_rows = slot_rows // count

    def saved_copies(s):
        return pltpu.make_async_copy(hidden_hbm.at[:, slots_ref[begin + s]], saved.at[:, s], saved_sem.at[s])

    @pl.when(expert == 0)
    def _():
        for copy in part_copies(parts, rows, part_sem):
            copy.start()
        each(count, lambda s: saved_copies(s).start())
        for copy in part_copies(parts, rows, part_sem):
            copy.wait()
        base = lax.axis_index("expert") * experts_here
        row, lane = iota((8, LANES), 0), iota((8, LANES), 1)
        wanted = base + jnp.where(row < experts_here, row, row - experts_here + LANES // 2)
        chosen = ((lane == wanted) & (row < 2 * experts_here)).astype(F32).astype(BF16)

        def look_up(s):
            at = pl.multiple_of(s * tokens, tokens)
            table_ref[s] = dot(chosen, rows[pl.ds(at, tokens), columns : columns + tokens])

        each(count, look_up)
        fill_slots(rows, routed, [table_ref], count)
        each(count, lambda s: saved_copies(s).wait())

    routed_ref[0] = routed[expert]
    if shares:
        product_ref[0] = dot(routed[expert], joined(weight_refs), ((1,), (1,))).astype(BF16)

    def weigh(s):
        hit, prob = hits(table_ref[s], expert, experts_here, cap)
        of_slot = jnp.sum(jnp.where(hit, prob, 0.0), axis=1, keepdims=True)
        scaled = of_slot * saved[expert, s].astype(F32)
        if cap_rows > cap:
            scaled = jnp.concatenate([scaled, jnp.zeros((cap_rows - cap, units), F32)], axis=0)
        weighted_ref[0, pl.ds(pl.multiple_of(s * cap_rows, cap_rows), cap_rows), :] = scaled.astype(BF16)

    each(count, weigh)


def visit(parts, slots, begin, weight, hidden, replicas, tokens, with_product=True):
    experts_here, _, cap, units = hidden.shape
    cap_rows = -(-cap // 16) * 16
    count = sum(part.shape[0] for part in parts) // tokens
    slot_rows = count * cap_rows
    columns = parts[0].shape[1] - tokens
    shares = weight_share(weight, columns, replicas, 0) if with_product else []
    product = jax.ShapeDtypeStruct((experts_here, slot_rows, units), BF16)
    routed = jax.ShapeDtypeStruct((experts_here, slot_rows, columns), BF16)
    table = jax.ShapeDtypeStruct((count, 8, tokens), F32)
    return pl.pallas_call(
        functools.partial(visit_kernel, len(parts), len(shares), begin),
        grid=(experts_here,),
        in_specs=[SMEM] + [HBM] * len(parts) + shares + [HBM],
        out_specs=[whole(routed), whole(product), pl.BlockSpec(table.shape, lambda e: (0, 0, 0))]
        + [whole(product)] * with_product,
        out_shape=[routed, product, table] + [product] * with_product,
        scratch_shapes=[
            pltpu.VMEM((count * tokens, parts[0].shape[1]), BF16),
            pltpu.VMEM((experts_here, slot_rows, columns), BF16),
            pltpu.VMEM((experts_here, count, cap, units), BF16),
            pltpu.SemaphoreType.DMA((len(parts),)),
            pltpu.SemaphoreType.DMA((count,)),
        ],
        compiler_params=params(),
        name="visit",
    )(slots, *parts, *[weight] * len(shares), hidden)


def owners(replicas):
    place = lax.axis_index("dp")
    groups = replicas // CORES
    chip, core = place // CORES, place % CORES
    away = [(chip + j + 1) % groups * CORES for j in range(groups)]
    return jnp.stack([at + 1 - core for at in away] + [at + core for at in away]).astype(jnp.int32)


def store_bands(taken, weighted_refs, outs):
    weighted = jnp.concatenate([ref[0] for ref in weighted_refs], axis=0)
    made = dot(taken, weighted, ((0,), (0,))).astype(BF16)
    at = 0
    for out_ref in outs:
        out_ref[...] = made[at : at + out_ref.shape[0], :]
        at += out_ref.shape[0]


def band_outputs(bands, width, experts_here, units):
    rows = [len(band) * width for band in bands]
    rows = [rows[0] // 2, rows[0] // 2] + rows[1:]
    specs = [pl.BlockSpec((size, units), lambda e, *_: (0, e)) for size in rows]
    shapes = [jax.ShapeDtypeStruct((size, experts_here * units), BF16) for size in rows]
    return specs, shapes


def bands_kernel(total, groups_here, weighted_here, owners_ref, *refs):
    taken = [
        jnp.concatenate([ref[0] for ref in refs[j * groups_here : (j + 1) * groups_here]], axis=0)
        for j in range(total)
    ]
    refs = refs[total * groups_here :]
    store_bands(jnp.concatenate(taken, axis=1), refs[:weighted_here], refs[weighted_here:])


def grad_bands(routed, weighted, owned, bands):
    experts_here, _, units = weighted[0].shape
    width = routed[0].shape[2] // owned.shape[0]
    wanted = [j for band in bands for j in band]
    out_specs, out_shape = band_outputs(bands, width, experts_here, units)

    def share(part, j):
        return pl.BlockSpec((1, part.shape[1], width), lambda e, owned: (e, 0, owned[j]))

    return pl.pallas_call(
        functools.partial(bands_kernel, len(wanted), len(routed), len(weighted)),
        grid_spec=pltpu.PrefetchScalarGridSpec(
            num_scalar_prefetch=1,
            grid=(experts_here,),
            in_specs=[share(part, j) for j in wanted for part in routed] + [whole(part) for part in weighted],
            out_specs=out_specs,
        ),
        out_shape=out_shape,
        compiler_params=params(),
        name="bands",
    )(owned, *[part for _ in wanted for part in routed], *weighted)


def route_kernel(parts_here, groups_here, wanted, width, owners_ref, *refs):
    parts, refs = refs[:parts_here], refs[parts_here:]
    tables, refs = refs[:groups_here], refs[groups_here:]
    weighted, refs = refs[:groups_here], refs[groups_here:]
    outs, (routed_hbm, rows, routed, part_sem, out_sem) = refs[:-5], refs[-5:]
    expert = pl.program_id(0)
    keep = pltpu.make_async_copy(routed, routed_hbm, out_sem)

    @pl.when(expert == 0)
    def _():
        for copy in part_copies(parts, rows, part_sem):
            copy.start()
        for copy in part_copies(parts, rows, part_sem):
            copy.wait()
        fill_slots(rows, routed, tables, sum(table.shape[0] for table in tables))
        keep.start()

    taken = [routed[expert, :, pl.ds(pl.multiple_of(owners_ref[j] * width, LANES), width)] for j in wanted]
    store_bands(jnp.concatenate(taken, axis=1), weighted, outs)

    @pl.when(expert == pl.num_programs(0) - 1)
    def _():
        keep.wait()


def route(parts, tables, weighted, owned, bands):
    experts_here, _, units = weighted[0].shape
    slot_rows = sum(part.shape[1] for part in weighted)
    token_rows, tokens = sum(part.shape[0] for part in parts), tables[0].shape[2]
    columns = parts[0].shape[1]
    width = columns // owned.shape[0]
    out_specs, out_shape = band_outputs(bands, width, experts_here, units)
    wanted = [j for band in bands for j in band]
    return pl.pallas_call(
        functools.partial(route_kernel, len(parts), len(tables), wanted, width),
        grid=(experts_here,),
        in_specs=[SMEM]
        + [HBM] * len(parts)
        + [pl.BlockSpec(table.shape, lambda e: (0, 0, 0)) for table in tables]
        + [whole(part) for part in weighted],
        out_specs=out_specs + [HBM],
        out_shape=out_shape + [jax.ShapeDtypeStruct((experts_here, slot_rows, columns), BF16)],
        scratch_shapes=[
            pltpu.VMEM((token_rows, columns), BF16),
            pltpu.VMEM((experts_here, slot_rows, columns), BF16),
            pltpu.SemaphoreType.DMA((len(parts),)),
            pltpu.SemaphoreType.DMA,
        ],
        compiler_params=params(),
        cost_estimate=pl.CostEstimate(
            flops=2 * experts_here * slot_rows * columns * (units + tokens), bytes_accessed=10_000_000, transcendentals=0
        ),
        name="route",
    )(owned, *parts, *tables, *weighted)


def back_kernel(shares, seen_here, late_here, groups_here, slots_ref, routed_ref, *refs):
    last_weights, refs = refs[:shares], refs[shares:]
    first_weights, refs = refs[: shares * late_here], refs[shares * late_here :]
    late, refs = refs[:late_here], refs[late_here:]
    seen, refs = refs[:seen_here], refs[seen_here:]
    tables, refs = refs[:groups_here], refs[groups_here:]
    hidden_ref, grad_ref, prob_ref, held = refs
    expert = pl.program_id(0)
    experts_here = pl.num_programs(0)
    _, sources, cap, units = hidden_ref.shape
    cap_rows = held.shape[0] // sources
    before = [ref[0].astype(F32) for ref in seen]
    before += [dot(ref[0], joined(first_weights), ((1,), (1,))) for ref in late]
    held[...] = dot(routed_ref[0], joined(last_weights), ((1,), (1,))) + jnp.concatenate(before, axis=0)

    def finish(first, table_ref, s):
        at = first + s
        source = slots_ref[at]
        mine = held[pl.ds(pl.multiple_of(at * cap_rows, cap_rows), cap), :]
        hit, prob = hits(table_ref[s], expert, experts_here, cap)
        of_slot = jnp.sum(jnp.where(hit, prob, 0.0), axis=1, keepdims=True)
        grad_ref[0, pl.ds(source, 1)] = (of_slot * mine).astype(BF16)[None]
        inner = jnp.sum(mine * hidden_ref[0, source].astype(F32), axis=1, keepdims=True)
        gate = jnp.sum(jnp.where(hit, inner, 0.0), axis=0, keepdims=True)
        prob_ref[pl.ds(source, 1), pl.ds(expert, 1), :] = gate[None]

    first = 0
    for table_ref in tables:
        each(table_ref.shape[0], functools.partial(finish, first, table_ref))
        first += table_ref.shape[0]


def back(routed, slots, weight, hidden, start, replicas, seen, late, tables):
    experts_here, sources, cap, units = hidden.shape
    columns = routed.shape[2]
    tokens = tables[0].shape[2]
    saved = pl.BlockSpec((1, sources, cap, units), lambda e: (e, 0, 0, 0))
    return pl.pallas_call(
        functools.partial(back_kernel, replicas, len(seen), len(late), len(tables)),
        grid=(experts_here,),
        in_specs=[SMEM, whole(routed)]
        + weight_share(weight, columns, replicas, start)
        + weight_share(weight, columns, replicas, 0) * len(late)
        + [whole(part) for part in late]
        + [whole(part) for part in seen]
        + [pl.BlockSpec(table.shape, lambda e: (0, 0, 0)) for table in tables]
        + [saved],
        out_specs=[saved, pl.BlockSpec((sources, experts_here, tokens), lambda e: (0, 0, 0))],
        out_shape=[
            jax.ShapeDtypeStruct(hidden.shape, BF16),
            jax.ShapeDtypeStruct((sources, experts_here, tokens), F32),
        ],
        scratch_shapes=[pltpu.VMEM((routed.shape[1], units), F32)],
        compiler_params=params(),
        name="back",
    )(slots, routed, *[weight] * (replicas * (1 + len(late))), *late, *seen, *tables, hidden)


def rotate_kernel(count, experts_here, turn_ref, *refs):
    parts, out_ref = refs[:count], refs[-1]
    units = parts[0].shape[1] // experts_here
    total = parts[0][...].astype(F32)
    for ref in parts[1:]:
        total = total + ref[...].astype(F32)
    side = jnp.concatenate([total[:, e * units : (e + 1) * units] for e in range(experts_here)], axis=0)
    high = side.astype(BF16)
    low = (side - high.astype(F32)).astype(BF16)
    turn = turn_ref[0]
    turned = (dot(turn, high) + dot(turn, low)) * (1.0 / math.sqrt(BLOCK))
    out_ref[...] = turned.reshape(out_ref.shape)


def rotate(parts, turns, first_block, rows_out, experts_here, filled):
    rows, lines = parts[0].shape
    units = lines // experts_here
    extra = [] if filled is None else [filled]
    return pl.pallas_call(
        functools.partial(rotate_kernel, len(parts), experts_here),
        grid=(rows // BLOCK,),
        in_specs=[pl.BlockSpec((1,) + turns.shape[1:], lambda b: (first_block + b, 0, 0))]
        + [pl.BlockSpec((BLOCK, lines), lambda b: (b, 0)) for _ in parts]
        + [ANY] * len(extra),
        out_specs=pl.BlockSpec((BLOCK, experts_here, units), lambda b: (first_block + b, 0, 0)),
        out_shape=jax.ShapeDtypeStruct((rows_out, experts_here, units), F32),
        input_output_aliases={1 + len(parts): 0} if extra else {},
        compiler_params=params(),
        name="rotate",
    )(turns, *parts, *extra)


def turn_matrices(sign_seed, rows_own, experts_here):
    row = jnp.arange(BLOCK * experts_here, dtype=jnp.int32)
    anded = (row // experts_here)[:, None] & (row % BLOCK)[None, :]
    parity = sum(((anded >> shift) & 1) for shift in range(BLOCK.bit_length() - 1)) & 1
    same = (row % experts_here)[:, None] == (row // BLOCK)[None, :]
    matrix = jnp.where(same, 1 - 2 * parity, 0)
    own = lax.dynamic_slice_in_dim(2 * sign_seed - 1, lax.axis_index("dp") * rows_own, rows_own)
    signs = jnp.tile(own.reshape(-1, 1, BLOCK), (1, 1, experts_here))
    return (matrix[None] * signs).astype(BF16)


def shards(cotangent, gate_prob, routes, hidden, down_weight, sign_seed):
    tokens, features = cotangent.shape
    sources, replicas = lax.axis_size("expert"), lax.axis_size("dp")
    groups = replicas // CORES
    experts_here, units = down_weight.shape[0], down_weight.shape[1]
    rows_own = features // replicas
    saved = hidden[0]
    cap = saved.shape[2]
    width = rows_own // 2
    pieces = [(0, width), (width, width)]
    turns = turn_matrices(sign_seed, rows_own, experts_here)
    sent = pack(cotangent, gate_prob, routes, pieces, replicas)
    owned = owners(replicas)
    away_bands = [tuple(range(groups - 1)), tuple(range(groups, 2 * groups - 1))]
    here_bands = [(groups - 1,), (2 * groups - 1,)]

    def swap(value):
        return lax.ppermute(value, "dp", [(i, i ^ 1) for i in range(replicas)])

    def to_chips(value):
        moved = []
        for k in range(1, groups):
            pairs = [(i, (i // CORES + k) % groups * CORES + i % CORES) for i in range(replicas)]
            moved.append(lax.ppermute(value[(k - 1) * width : k * width], "dp", pairs))
        return moved

    def add_swapped(halves, kept):
        got = jnp.concatenate([swap(half) for half in halves], axis=0)
        return (got.astype(F32) + kept.astype(F32)).astype(BF16)

    def visit_first(parts, begin, with_product=True):
        return visit(parts, slots, begin, down_weight, saved, replicas, tokens, with_product)

    def bands_first(visits, bands):
        return grad_bands([made[0] for made in visits], [made[1] for made in visits], owned, bands)

    a, b = sent
    if sources == 2 * LINES:
        a_x, b_x, a_next, a_prev, a, b, turns, owned, slots = fence(
            across(a), across(b), along(a, 1), along(a, -1), a, b, turns, owned, line_slots()
        )
        a_opp, a_xnext, a_xprev = along(a, 2), across(a_next), across(a_prev)
        a_near = visit_first([a, a_x, a_next, a_prev], 0)
        a_opp, a_xnext, a_xprev, a_near, b = fence(a_opp, a_xnext, a_xprev, a_near, b)
        a_xopp, b_next, b_prev = across(a_opp), along(b, 1), along(b, -1)
        a_far = visit_first([a_opp, a_xnext, a_xprev], 4)
        a_xopp, b_next, b_prev, a_far, b = fence(a_xopp, b_next, b_prev, a_far, b)
        b_opp, b_xnext, b_xprev = along(b, 2), across(b_next), across(b_prev)
        a_made = [a_near, a_far, visit_first([a_xopp], 7, with_product=False)]
        made = bands_first(a_made, away_bands + here_bands)
        b_opp, b_xnext, b_xprev, made = fence(b_opp, b_xnext, b_xprev, made)
        *away_send, away_keep, here_send, here_keep = made
        b_xopp = across(b_opp)
        a_arrived = to_chips(add_swapped(away_send, away_keep))
        b_xopp, here_send = fence(b_xopp, here_send)
        b_parts = [b, b_x, b_next, b_prev, b_opp, b_xnext, b_xprev, b_xopp]
        seen, late = [a_near[3], a_far[3]], [a_made[2][0]]
    else:
        a, b = [lax.all_gather(part, "expert", axis=0, tiled=True) for part in sent]
        slots = jnp.arange(sources, dtype=jnp.int32)
        a_made = [visit_first([a], 0)]
        *away_send, away_keep, here_send, here_keep = bands_first(a_made, away_bands + here_bands)
        a_arrived = to_chips(add_swapped(away_send, away_keep))
        b_parts = [b]
        seen, late = [a_made[0][3]], []

    weighted = [made[1] for made in a_made]
    tables = [made[2] for made in a_made]
    made = route(b_parts, tables, weighted, owned, away_bands + here_bands)
    *away_send, away_keep, here_send_b, here_keep_b, routed_b = made
    away_keep, a_arrived = fence(away_keep, a_arrived)
    b_arrived = to_chips(add_swapped(away_send, away_keep))
    here_got, here_got_b = swap(here_send), swap(here_send_b)
    grad_hidden, grad_slots = back(routed_b, slots, down_weight, saved, width, replicas, seen, late, tables)
    returned = lax.all_to_all(grad_slots, "expert", split_axis=0, concat_axis=0, tiled=True)
    out = rotate([here_keep, here_got] + a_arrived, turns, 0, rows_own, experts_here, None)
    out, *b_arrived = fence(out, *b_arrived)
    out = rotate([here_keep_b, here_got_b] + b_arrived, turns, width // BLOCK, rows_own, experts_here, out)
    returned, out = fence(returned, out)
    of_token = returned.reshape(-1, 1, tokens)
    named = routes.T[None] == jnp.arange(of_token.shape[0], dtype=jnp.int32)[:, None, None]
    grad_prob = jnp.sum(jnp.where(named, of_token, 0.0), axis=0).T
    return (grad_hidden[None], grad_prob, out)


def solution(mesh):
    in_specs = (
        P(("dp", "expert"), None),
        P(("dp", "expert"), None),
        P(("dp", "expert"), None),
        P("dp", "expert", None, None, None),
        P("expert", None, None),
        P(),
    )
    out_specs = (
        P("dp", "expert", None, None, None),
        P(("dp", "expert"), None),
        P("dp", "expert", None),
    )
    return jax.shard_map(shards, mesh=mesh, in_specs=in_specs, out_specs=out_specs, check_vma=False)
```

```python
import functools
import math

import jax
import jax.numpy as jnp
from jax import lax
from jax.experimental import pallas as pl
from jax.experimental.pallas import tpu as pltpu
from jax.sharding import PartitionSpec as P

BLOCK = 128
LANES = 128
CORES = 2
NO_SLOT = 512.0
VMEM = 32 * 1024 * 1024
F32 = jnp.float32
BF16 = jnp.bfloat16


ANY = pl.BlockSpec(memory_space=pl.ANY)
HBM = pl.BlockSpec(memory_space=pltpu.HBM)
SMEM = pl.BlockSpec(memory_space=pltpu.SMEM)


def params(limit=VMEM):
    return pltpu.CompilerParams(vmem_limit_bytes=limit)


def dot(a, b, contract=((1,), (0,))):
    return lax.dot_general(a, b, (contract, ((), ())), preferred_element_type=F32)


def iota(shape, axis):
    return lax.broadcasted_iota(jnp.int32, shape, axis)


def pack_kernel(pieces, replicas, cot_ref, gate_ref, route_ref, *out_refs):
    rows_own = cot_ref.shape[1] // replicas
    for out_ref, (start, width) in zip(out_refs, pieces):
        for q in range(replicas):
            at = q * rows_own + start
            out_ref[:, q * width : (q + 1) * width] = cot_ref[:, at : at + width]
    tokens = cot_ref.shape[0]
    line = iota((LANES, tokens), 0)
    half = LANES // 2
    gate = jnp.zeros((LANES, tokens), F32)
    hit = jnp.zeros((LANES, tokens), F32)
    for k in range(route_ref.shape[0]):
        named = route_ref[k : k + 1, :]
        gate = gate + jnp.where(named == line, gate_ref[k : k + 1, :].astype(F32), 0.0)
        hit = hit + jnp.where(named == line - half, 1.0, 0.0)
    earlier = (iota((tokens, tokens), 0) < iota((tokens, tokens), 1)).astype(F32).astype(BF16)
    rank = dot(hit.astype(BF16), earlier)
    table = jnp.where(line < half, gate, jnp.where(hit > 0, rank, NO_SLOT))
    first = out_refs[0]
    first[:, first.shape[1] - tokens :] = table.astype(BF16)


def pack(cotangent, gate_prob, routes, pieces, replicas):
    tokens = cotangent.shape[0]
    widths = [replicas * width for _, width in pieces]
    widths[0] += tokens
    return pl.pallas_call(
        functools.partial(pack_kernel, pieces, replicas),
        out_shape=[jax.ShapeDtypeStruct((tokens, width), BF16) for width in widths],
        compiler_params=params(),
        name="pack",
    )(cotangent, gate_prob.T, routes.T)


LINES = 4


def along(value, by):
    pairs = [(line, (line + by) % LINES) for line in range(LINES)]
    return lax.ppermute(value, "expert", [(2 * a + x, 2 * b + x) for a, b in pairs for x in (0, 1)])


def across(value):
    return lax.ppermute(value, "expert", [(i, i ^ 1) for i in range(2 * LINES)])


def fence(*values):
    return lax.optimization_barrier(values)


def line_slots():
    place = lax.axis_index("expert")
    line, side = place // 2, place % 2
    before, behind, facing = (line + LINES - 1) % LINES, (line + 1) % LINES, (line + 2) % LINES
    near = [2 * line + side, 2 * line + 1 - side, 2 * before + side, 2 * behind + side]
    far = [2 * facing + side, 2 * before + 1 - side, 2 * behind + 1 - side]
    farthest = [2 * facing + 1 - side]
    return jnp.stack(near + far + farthest).astype(jnp.int32)


def hits(table, expert, experts_here, cap_rows):
    line = iota(table.shape, 0)
    rank = jnp.sum(jnp.where(line == experts_here + expert, table, 0.0), axis=0, keepdims=True)
    prob = jnp.sum(jnp.where(line == expert, table, 0.0), axis=0, keepdims=True)
    return iota((cap_rows, table.shape[1]), 0).astype(F32) == rank, prob


def fill_slots(rows, routed, tables, sources):
    experts_here, slot_rows, columns = routed.shape
    cap_rows = slot_rows // sources
    tokens = rows.shape[0] // sources

    def fill(first, table_ref, s):
        table = table_ref[s]
        picked = [hits(table, e, experts_here, cap_rows)[0].astype(F32).astype(BF16) for e in range(experts_here)]
        at = pl.multiple_of((first + s) * tokens, tokens)
        got = dot(jnp.concatenate(picked, axis=0), rows[pl.ds(at, tokens), :columns]).astype(BF16)
        to = pl.multiple_of((first + s) * cap_rows, cap_rows)
        for e in range(experts_here):
            routed[e, pl.ds(to, cap_rows), :] = got[e * cap_rows : (e + 1) * cap_rows, :]

    first = 0
    for table_ref in tables:
        each(table_ref.shape[0], functools.partial(fill, first, table_ref))
        first += table_ref.shape[0]


def each(count, body):
    def step(s, carry):
        body(s)
        return carry

    lax.fori_loop(0, count, step, 0, unroll=count <= 8)


def part_copies(parts, rows, sem):
    size = rows.shape[0] // len(parts)
    return [
        pltpu.make_async_copy(part, rows.at[pl.ds(i * size, size), :], sem.at[i]) for i, part in enumerate(parts)
    ]


def whole(part):
    return pl.BlockSpec((1,) + part.shape[1:], lambda e, *_: (e, 0, 0))


def weight_share(weight, columns, replicas, start):
    units, features = weight.shape[1:]
    width, rows_own = columns // replicas, features // replicas

    def share(q):
        return pl.BlockSpec((1, units, width), lambda e: (e, 0, (q * rows_own + start) // width))

    return [share(q) for q in range(replicas)]


def joined(refs):
    return jnp.concatenate([ref[0] for ref in refs], axis=1)


def visit_kernel(parts_here, shares, begin, slots_ref, *refs):
    parts, refs = refs[:parts_here], refs[parts_here:]
    weight_refs, refs = refs[:shares], refs[shares:]
    hidden_hbm, routed_ref, weighted_ref, table_ref = refs[:4]
    product_ref = refs[4] if shares else None
    rows, routed, saved, part_sem, saved_sem = refs[-5:]
    expert = pl.program_id(0)
    experts_here, slot_rows, columns = routed.shape
    _, count, cap, units = saved.shape
    tokens = table_ref.shape[2]
    cap_rows = slot_rows // count

    def saved_copies(s):
        return pltpu.make_async_copy(hidden_hbm.at[:, slots_ref[begin + s]], saved.at[:, s], saved_sem.at[s])

    @pl.when(expert == 0)
    def _():
        for copy in part_copies(parts, rows, part_sem):
            copy.start()
        each(count, lambda s: saved_copies(s).start())
        for copy in part_copies(parts, rows, part_sem):
            copy.wait()
        base = lax.axis_index("expert") * experts_here
        row, lane = iota((8, LANES), 0), iota((8, LANES), 1)
        wanted = base + jnp.where(row < experts_here, row, row - experts_here + LANES // 2)
        chosen = ((lane == wanted) & (row < 2 * experts_here)).astype(F32).astype(BF16)

        def look_up(s):
            at = pl.multiple_of(s * tokens, tokens)
            table_ref[s] = dot(chosen, rows[pl.ds(at, tokens), columns : columns + tokens])

        each(count, look_up)
        fill_slots(rows, routed, [table_ref], count)
        each(count, lambda s: saved_copies(s).wait())

    routed_ref[0] = routed[expert]
    if shares:
        product_ref[0] = dot(routed[expert], joined(weight_refs), ((1,), (1,))).astype(BF16)

    def weigh(s):
        hit, prob = hits(table_ref[s], expert, experts_here, cap)
        of_slot = jnp.sum(jnp.where(hit, prob, 0.0), axis=1, keepdims=True)
        scaled = of_slot * saved[expert, s].astype(F32)
        if cap_rows > cap:
            scaled = jnp.concatenate([scaled, jnp.zeros((cap_rows - cap, units), F32)], axis=0)
        weighted_ref[0, pl.ds(pl.multiple_of(s * cap_rows, cap_rows), cap_rows), :] = scaled.astype(BF16)

    each(count, weigh)


def visit(parts, slots, begin, weight, hidden, replicas, tokens, with_product=True):
    experts_here, _, cap, units = hidden.shape
    cap_rows = -(-cap // 16) * 16
    count = sum(part.shape[0] for part in parts) // tokens
    slot_rows = count * cap_rows
    columns = parts[0].shape[1] - tokens
    shares = weight_share(weight, columns, replicas, 0) if with_product else []
    product = jax.ShapeDtypeStruct((experts_here, slot_rows, units), BF16)
    routed = jax.ShapeDtypeStruct((experts_here, slot_rows, columns), BF16)
    table = jax.ShapeDtypeStruct((count, 8, tokens), F32)
    return pl.pallas_call(
        functools.partial(visit_kernel, len(parts), len(shares), begin),
        grid=(experts_here,),
        in_specs=[SMEM] + [HBM] * len(parts) + shares + [HBM],
        out_specs=[whole(routed), whole(product), pl.BlockSpec(table.shape, lambda e: (0, 0, 0))]
        + [whole(product)] * with_product,
        out_shape=[routed, product, table] + [product] * with_product,
        scratch_shapes=[
            pltpu.VMEM((count * tokens, parts[0].shape[1]), BF16),
            pltpu.VMEM((experts_here, slot_rows, columns), BF16),
            pltpu.VMEM((experts_here, count, cap, units), BF16),
            pltpu.SemaphoreType.DMA((len(parts),)),
            pltpu.SemaphoreType.DMA((count,)),
        ],
        compiler_params=params(),
        name="visit",
    )(slots, *parts, *[weight] * len(shares), hidden)


def owners(replicas):
    place = lax.axis_index("dp")
    groups = replicas // CORES
    chip, core = place // CORES, place % CORES
    away = [(chip + j + 1) % groups * CORES for j in range(groups)]
    return jnp.stack([at + 1 - core for at in away] + [at + core for at in away]).astype(jnp.int32)


def store_bands(taken, weighted_refs, outs):
    weighted = jnp.concatenate([ref[0] for ref in weighted_refs], axis=0)
    made = dot(taken, weighted, ((0,), (0,))).astype(BF16)
    at = 0
    for out_ref in outs:
        out_ref[...] = made[at : at + out_ref.shape[0], :]
        at += out_ref.shape[0]


def band_outputs(bands, width, experts_here, units):
    rows = [len(band) * width for band in bands]
    rows = [rows[0] // 2, rows[0] // 2] + rows[1:]
    specs = [pl.BlockSpec((size, units), lambda e, *_: (0, e)) for size in rows]
    shapes = [jax.ShapeDtypeStruct((size, experts_here * units), BF16) for size in rows]
    return specs, shapes


def bands_kernel(total, groups_here, weighted_here, owners_ref, *refs):
    taken = [
        jnp.concatenate([ref[0] for ref in refs[j * groups_here : (j + 1) * groups_here]], axis=0)
        for j in range(total)
    ]
    refs = refs[total * groups_here :]
    store_bands(jnp.concatenate(taken, axis=1), refs[:weighted_here], refs[weighted_here:])


def grad_bands(routed, weighted, owned, bands):
    experts_here, _, units = weighted[0].shape
    width = routed[0].shape[2] // owned.shape[0]
    wanted = [j for band in bands for j in band]
    out_specs, out_shape = band_outputs(bands, width, experts_here, units)

    def share(part, j):
        return pl.BlockSpec((1, part.shape[1], width), lambda e, owned: (e, 0, owned[j]))

    return pl.pallas_call(
        functools.partial(bands_kernel, len(wanted), len(routed), len(weighted)),
        grid_spec=pltpu.PrefetchScalarGridSpec(
            num_scalar_prefetch=1,
            grid=(experts_here,),
            in_specs=[share(part, j) for j in wanted for part in routed] + [whole(part) for part in weighted],
            out_specs=out_specs,
        ),
        out_shape=out_shape,
        compiler_params=params(),
        name="bands",
    )(owned, *[part for _ in wanted for part in routed], *weighted)


def route_kernel(parts_here, groups_here, wanted, width, owners_ref, *refs):
    parts, refs = refs[:parts_here], refs[parts_here:]
    tables, refs = refs[:groups_here], refs[groups_here:]
    weighted, refs = refs[:groups_here], refs[groups_here:]
    outs, (routed_hbm, rows, routed, part_sem, out_sem) = refs[:-5], refs[-5:]
    expert = pl.program_id(0)
    keep = pltpu.make_async_copy(routed, routed_hbm, out_sem)

    @pl.when(expert == 0)
    def _():
        for copy in part_copies(parts, rows, part_sem):
            copy.start()
        for copy in part_copies(parts, rows, part_sem):
            copy.wait()
        fill_slots(rows, routed, tables, sum(table.shape[0] for table in tables))
        keep.start()

    taken = [routed[expert, :, pl.ds(pl.multiple_of(owners_ref[j] * width, LANES), width)] for j in wanted]
    store_bands(jnp.concatenate(taken, axis=1), weighted, outs)

    @pl.when(expert == pl.num_programs(0) - 1)
    def _():
        keep.wait()


def route(parts, tables, weighted, owned, bands):
    experts_here, _, units = weighted[0].shape
    slot_rows = sum(part.shape[1] for part in weighted)
    token_rows, tokens = sum(part.shape[0] for part in parts), tables[0].shape[2]
    columns = parts[0].shape[1]
    width = columns // owned.shape[0]
    out_specs, out_shape = band_outputs(bands, width, experts_here, units)
    wanted = [j for band in bands for j in band]
    return pl.pallas_call(
        functools.partial(route_kernel, len(parts), len(tables), wanted, width),
        grid=(experts_here,),
        in_specs=[SMEM]
        + [HBM] * len(parts)
        + [pl.BlockSpec(table.shape, lambda e: (0, 0, 0)) for table in tables]
        + [whole(part) for part in weighted],
        out_specs=out_specs + [HBM],
        out_shape=out_shape + [jax.ShapeDtypeStruct((experts_here, slot_rows, columns), BF16)],
        scratch_shapes=[
            pltpu.VMEM((token_rows, columns), BF16),
            pltpu.VMEM((experts_here, slot_rows, columns), BF16),
            pltpu.SemaphoreType.DMA((len(parts),)),
            pltpu.SemaphoreType.DMA,
        ],
        compiler_params=params(),
        cost_estimate=pl.CostEstimate(
            flops=2 * experts_here * slot_rows * columns * (units + tokens), bytes_accessed=10_000_000, transcendentals=0
        ),
        name="route",
    )(owned, *parts, *tables, *weighted)


def back_kernel(shares, seen_here, late_here, groups_here, slots_ref, routed_ref, *refs):
    last_weights, refs = refs[:shares], refs[shares:]
    first_weights, refs = refs[: shares * late_here], refs[shares * late_here :]
    late, refs = refs[:late_here], refs[late_here:]
    seen, refs = refs[:seen_here], refs[seen_here:]
    tables, refs = refs[:groups_here], refs[groups_here:]
    hidden_ref, grad_ref, prob_ref, held = refs
    expert = pl.program_id(0)
    experts_here = pl.num_programs(0)
    _, sources, cap, units = hidden_ref.shape
    cap_rows = held.shape[0] // sources
    before = [ref[0].astype(F32) for ref in seen]
    before += [dot(ref[0], joined(first_weights), ((1,), (1,))) for ref in late]
    held[...] = dot(routed_ref[0], joined(last_weights), ((1,), (1,))) + jnp.concatenate(before, axis=0)

    def finish(first, table_ref, s):
        at = first + s
        source = slots_ref[at]
        mine = held[pl.ds(pl.multiple_of(at * cap_rows, cap_rows), cap), :]
        hit, prob = hits(table_ref[s], expert, experts_here, cap)
        of_slot = jnp.sum(jnp.where(hit, prob, 0.0), axis=1, keepdims=True)
        grad_ref[0, pl.ds(source, 1)] = (of_slot * mine).astype(BF16)[None]
        inner = jnp.sum(mine * hidden_ref[0, source].astype(F32), axis=1, keepdims=True)
        gate = jnp.sum(jnp.where(hit, inner, 0.0), axis=0, keepdims=True)
        prob_ref[pl.ds(source, 1), pl.ds(expert, 1), :] = gate[None]

    first = 0
    for table_ref in tables:
        each(table_ref.shape[0], functools.partial(finish, first, table_ref))
        first += table_ref.shape[0]


def back(routed, slots, weight, hidden, start, replicas, seen, late, tables):
    experts_here, sources, cap, units = hidden.shape
    columns = routed.shape[2]
    tokens = tables[0].shape[2]
    saved = pl.BlockSpec((1, sources, cap, units), lambda e: (e, 0, 0, 0))
    return pl.pallas_call(
        functools.partial(back_kernel, replicas, len(seen), len(late), len(tables)),
        grid=(experts_here,),
        in_specs=[SMEM, whole(routed)]
        + weight_share(weight, columns, replicas, start)
        + weight_share(weight, columns, replicas, 0) * len(late)
        + [whole(part) for part in late]
        + [whole(part) for part in seen]
        + [pl.BlockSpec(table.shape, lambda e: (0, 0, 0)) for table in tables]
        + [saved],
        out_specs=[saved, pl.BlockSpec((sources, experts_here, tokens), lambda e: (0, 0, 0))],
        out_shape=[
            jax.ShapeDtypeStruct(hidden.shape, BF16),
            jax.ShapeDtypeStruct((sources, experts_here, tokens), F32),
        ],
        scratch_shapes=[pltpu.VMEM((routed.shape[1], units), F32)],
        compiler_params=params(),
        name="back",
    )(slots, routed, *[weight] * (replicas * (1 + len(late))), *late, *seen, *tables, hidden)


def rotate_kernel(count, experts_here, turn_ref, *refs):
    parts, out_ref = refs[:count], refs[-1]
    units = parts[0].shape[1] // experts_here
    total = parts[0][...].astype(F32)
    for ref in parts[1:]:
        total = total + ref[...].astype(F32)
    side = jnp.concatenate([total[:, e * units : (e + 1) * units] for e in range(experts_here)], axis=0)
    high = side.astype(BF16)
    low = (side - high.astype(F32)).astype(BF16)
    turn = turn_ref[0]
    turned = (dot(turn, high) + dot(turn, low)) * (1.0 / math.sqrt(BLOCK))
    out_ref[...] = turned.reshape(out_ref.shape)


def rotate(parts, turns, first_block, rows_out, experts_here, filled):
    rows, lines = parts[0].shape
    units = lines // experts_here
    extra = [] if filled is None else [filled]
    return pl.pallas_call(
        functools.partial(rotate_kernel, len(parts), experts_here),
        grid=(rows // BLOCK,),
        in_specs=[pl.BlockSpec((1,) + turns.shape[1:], lambda b: (first_block + b, 0, 0))]
        + [pl.BlockSpec((BLOCK, lines), lambda b: (b, 0)) for _ in parts]
        + [ANY] * len(extra),
        out_specs=pl.BlockSpec((BLOCK, experts_here, units), lambda b: (first_block + b, 0, 0)),
        out_shape=jax.ShapeDtypeStruct((rows_out, experts_here, units), F32),
        input_output_aliases={1 + len(parts): 0} if extra else {},
        compiler_params=params(),
        name="rotate",
    )(turns, *parts, *extra)


def turn_matrices(sign_seed, rows_own, experts_here):
    row = jnp.arange(BLOCK * experts_here, dtype=jnp.int32)
    anded = (row // experts_here)[:, None] & (row % BLOCK)[None, :]
    parity = sum(((anded >> shift) & 1) for shift in range(BLOCK.bit_length() - 1)) & 1
    same = (row % experts_here)[:, None] == (row // BLOCK)[None, :]
    matrix = jnp.where(same, 1 - 2 * parity, 0)
    own = lax.dynamic_slice_in_dim(2 * sign_seed - 1, lax.axis_index("dp") * rows_own, rows_own)
    signs = jnp.tile(own.reshape(-1, 1, BLOCK), (1, 1, experts_here))
    return (matrix[None] * signs).astype(BF16)


def shards(cotangent, gate_prob, routes, hidden, down_weight, sign_seed):
    tokens, features = cotangent.shape
    sources, replicas = lax.axis_size("expert"), lax.axis_size("dp")
    groups = replicas // CORES
    experts_here, units = down_weight.shape[0], down_weight.shape[1]
    rows_own = features // replicas
    saved = hidden[0]
    cap = saved.shape[2]
    width = rows_own // 2
    pieces = [(0, width), (width, width)]
    turns = turn_matrices(sign_seed, rows_own, experts_here)
    sent = pack(cotangent, gate_prob, routes, pieces, replicas)
    owned = owners(replicas)
    away_bands = [tuple(range(groups - 1)), tuple(range(groups, 2 * groups - 1))]
    here_bands = [(groups - 1,), (2 * groups - 1,)]

    def swap(value):
        return lax.ppermute(value, "dp", [(i, i ^ 1) for i in range(replicas)])

    def to_chips(value):
        moved = []
        for k in range(1, groups):
            pairs = [(i, (i // CORES + k) % groups * CORES + i % CORES) for i in range(replicas)]
            moved.append(lax.ppermute(value[(k - 1) * width : k * width], "dp", pairs))
        return moved

    def add_swapped(halves, kept):
        got = jnp.concatenate([swap(half) for half in halves], axis=0)
        return (got.astype(F32) + kept.astype(F32)).astype(BF16)

    def visit_first(parts, begin, with_product=True):
        return visit(parts, slots, begin, down_weight, saved, replicas, tokens, with_product)

    def bands_first(visits, bands):
        return grad_bands([made[0] for made in visits], [made[1] for made in visits], owned, bands)

    a, b = sent
    if sources == 2 * LINES:
        a_x, b_x, a_next, a_prev, a, b, turns, owned, slots = fence(
            across(a), across(b), along(a, 1), along(a, -1), a, b, turns, owned, line_slots()
        )
        a_opp, a_xnext, a_xprev = along(a, 2), across(a_next), across(a_prev)
        a_near = visit_first([a, a_x, a_next, a_prev], 0)
        a_opp, a_xnext, a_xprev, a_near, b = fence(a_opp, a_xnext, a_xprev, a_near, b)
        a_xopp, b_next, b_prev = across(a_opp), along(b, 1), along(b, -1)
        a_far = visit_first([a_opp, a_xnext, a_xprev], 4)
        a_xopp, a_far, b = fence(a_xopp, a_far, b)
        a_made = [a_near, a_far, visit_first([a_xopp], 7, with_product=False)]
        made = bands_first(a_made, away_bands + here_bands)
        b_next, b_prev, made, b = fence(b_next, b_prev, made, b)
        b_opp, b_xnext, b_xprev = along(b, 2), across(b_next), across(b_prev)
        *away_send, away_keep, here_send, here_keep = made
        b_opp, b_xnext, b_xprev = fence(b_opp, b_xnext, b_xprev)
        b_xopp = across(b_opp)
        a_arrived = to_chips(add_swapped(away_send, away_keep))
        b_xopp, here_send = fence(b_xopp, here_send)
        b_parts = [b, b_x, b_next, b_prev, b_opp, b_xnext, b_xprev, b_xopp]
        seen, late = [a_near[3], a_far[3]], [a_made[2][0]]
    else:
        a, b = [lax.all_gather(part, "expert", axis=0, tiled=True) for part in sent]
        slots = jnp.arange(sources, dtype=jnp.int32)
        a_made = [visit_first([a], 0)]
        *away_send, away_keep, here_send, here_keep = bands_first(a_made, away_bands + here_bands)
        a_arrived = to_chips(add_swapped(away_send, away_keep))
        b_parts = [b]
        seen, late = [a_made[0][3]], []

    weighted = [made[1] for made in a_made]
    tables = [made[2] for made in a_made]
    made = route(b_parts, tables, weighted, owned, away_bands + here_bands)
    made, a_arrived = fence(made, a_arrived)
    *away_send, away_keep, here_send_b, here_keep_b, routed_b = made
    b_arrived = to_chips(add_swapped(away_send, away_keep))
    here_got, here_got_b = swap(here_send), swap(here_send_b)
    grad_hidden, grad_slots = back(routed_b, slots, down_weight, saved, width, replicas, seen, late, tables)
    returned = lax.all_to_all(grad_slots, "expert", split_axis=0, concat_axis=0, tiled=True)
    out = rotate([here_keep, here_got] + a_arrived, turns, 0, rows_own, experts_here, None)
    out, *b_arrived = fence(out, *b_arrived)
    out = rotate([here_keep_b, here_got_b] + b_arrived, turns, width // BLOCK, rows_own, experts_here, out)
    returned, out = fence(returned, out)
    of_token = returned.reshape(-1, 1, tokens)
    named = routes.T[None] == jnp.arange(of_token.shape[0], dtype=jnp.int32)[:, None, None]
    grad_prob = jnp.sum(jnp.where(named, of_token, 0.0), axis=0).T
    return (grad_hidden[None], grad_prob, out)


def solution(mesh):
    in_specs = (
        P(("dp", "expert"), None),
        P(("dp", "expert"), None),
        P(("dp", "expert"), None),
        P("dp", "expert", None, None, None),
        P("expert", None, None),
        P(),
    )
    out_specs = (
        P("dp", "expert", None, None, None),
        P(("dp", "expert"), None),
        P("dp", "expert", None),
    )
    return jax.shard_map(shards, mesh=mesh, in_specs=in_specs, out_specs=out_specs, check_vma=False)
```

```python
import functools
import math

import jax
import jax.numpy as jnp
from jax import lax
from jax.experimental import pallas as pl
from jax.experimental.pallas import tpu as pltpu
from jax.sharding import PartitionSpec as P

BLOCK = 128
LANES = 128
CORES = 2
NO_SLOT = 512.0
VMEM = 32 * 1024 * 1024
F32 = jnp.float32
BF16 = jnp.bfloat16


ANY = pl.BlockSpec(memory_space=pl.ANY)
HBM = pl.BlockSpec(memory_space=pltpu.HBM)
SMEM = pl.BlockSpec(memory_space=pltpu.SMEM)


def params(limit=VMEM):
    return pltpu.CompilerParams(vmem_limit_bytes=limit)


def dot(a, b, contract=((1,), (0,))):
    return lax.dot_general(a, b, (contract, ((), ())), preferred_element_type=F32)


def iota(shape, axis):
    return lax.broadcasted_iota(jnp.int32, shape, axis)


def pack_kernel(pieces, replicas, cot_ref, gate_ref, route_ref, *out_refs):
    rows_own = cot_ref.shape[1] // replicas
    for out_ref, (start, width) in zip(out_refs, pieces):
        for q in range(replicas):
            at = q * rows_own + start
            out_ref[:, q * width : (q + 1) * width] = cot_ref[:, at : at + width]
    tokens = cot_ref.shape[0]
    line = iota((LANES, tokens), 0)
    half = LANES // 2
    gate = jnp.zeros((LANES, tokens), F32)
    hit = jnp.zeros((LANES, tokens), F32)
    for k in range(route_ref.shape[0]):
        named = route_ref[k : k + 1, :]
        gate = gate + jnp.where(named == line, gate_ref[k : k + 1, :].astype(F32), 0.0)
        hit = hit + jnp.where(named == line - half, 1.0, 0.0)
    earlier = (iota((tokens, tokens), 0) < iota((tokens, tokens), 1)).astype(F32).astype(BF16)
    rank = dot(hit.astype(BF16), earlier)
    table = jnp.where(line < half, gate, jnp.where(hit > 0, rank, NO_SLOT))
    first = out_refs[0]
    first[:, first.shape[1] - tokens :] = table.astype(BF16)


def pack(cotangent, gate_prob, routes, pieces, replicas):
    tokens = cotangent.shape[0]
    widths = [replicas * width for _, width in pieces]
    widths[0] += tokens
    return pl.pallas_call(
        functools.partial(pack_kernel, pieces, replicas),
        out_shape=[jax.ShapeDtypeStruct((tokens, width), BF16) for width in widths],
        compiler_params=params(56 * 1024 * 1024),
        name="pack",
    )(cotangent, gate_prob.T, routes.T)


LINES = 4


def along(value, by):
    pairs = [(line, (line + by) % LINES) for line in range(LINES)]
    return lax.ppermute(value, "expert", [(2 * a + x, 2 * b + x) for a, b in pairs for x in (0, 1)])


def across(value):
    return lax.ppermute(value, "expert", [(i, i ^ 1) for i in range(2 * LINES)])


def fence(*values):
    return lax.optimization_barrier(values)


def line_slots():
    place = lax.axis_index("expert")
    line, side = place // 2, place % 2
    before, behind, facing = (line + LINES - 1) % LINES, (line + 1) % LINES, (line + 2) % LINES
    near = [2 * line + side, 2 * line + 1 - side, 2 * before + side, 2 * behind + side]
    far = [2 * facing + side, 2 * before + 1 - side, 2 * behind + 1 - side]
    farthest = [2 * facing + 1 - side]
    return jnp.stack(near + far + farthest).astype(jnp.int32)


def hits(table, expert, experts_here, cap_rows):
    line = iota(table.shape, 0)
    rank = jnp.sum(jnp.where(line == experts_here + expert, table, 0.0), axis=0, keepdims=True)
    prob = jnp.sum(jnp.where(line == expert, table, 0.0), axis=0, keepdims=True)
    return iota((cap_rows, table.shape[1]), 0).astype(F32) == rank, prob


def fill_slots(rows, routed, tables, sources):
    experts_here, slot_rows, columns = routed.shape
    cap_rows = slot_rows // sources
    tokens = rows.shape[0] // sources

    def fill(first, table_ref, s):
        table = table_ref[s]
        picked = [hits(table, e, experts_here, cap_rows)[0].astype(F32).astype(BF16) for e in range(experts_here)]
        at = pl.multiple_of((first + s) * tokens, tokens)
        got = dot(jnp.concatenate(picked, axis=0), rows[pl.ds(at, tokens), :columns]).astype(BF16)
        to = pl.multiple_of((first + s) * cap_rows, cap_rows)
        for e in range(experts_here):
            routed[e, pl.ds(to, cap_rows), :] = got[e * cap_rows : (e + 1) * cap_rows, :]

    first = 0
    for table_ref in tables:
        each(table_ref.shape[0], functools.partial(fill, first, table_ref))
        first += table_ref.shape[0]


def each(count, body):
    def step(s, carry):
        body(s)
        return carry

    lax.fori_loop(0, count, step, 0, unroll=count <= 8)


def part_copies(parts, rows, sem):
    size = rows.shape[0] // len(parts)
    return [
        pltpu.make_async_copy(part, rows.at[pl.ds(i * size, size), :], sem.at[i]) for i, part in enumerate(parts)
    ]


def whole(part):
    return pl.BlockSpec((1,) + part.shape[1:], lambda e, *_: (e, 0, 0))


def weight_share(weight, columns, replicas, start):
    units, features = weight.shape[1:]
    width, rows_own = columns // replicas, features // replicas

    def share(q):
        return pl.BlockSpec((1, units, width), lambda e: (e, 0, (q * rows_own + start) // width))

    return [share(q) for q in range(replicas)]


def joined(refs):
    return jnp.concatenate([ref[0] for ref in refs], axis=1)


def visit_kernel(parts_here, shares, begin, slots_ref, *refs):
    parts, refs = refs[:parts_here], refs[parts_here:]
    weight_refs, refs = refs[:shares], refs[shares:]
    hidden_hbm, routed_ref, weighted_ref, table_ref = refs[:4]
    product_ref = refs[4] if shares else None
    rows, routed, saved, part_sem, saved_sem = refs[-5:]
    expert = pl.program_id(0)
    experts_here, slot_rows, columns = routed.shape
    _, count, cap, units = saved.shape
    tokens = table_ref.shape[2]
    cap_rows = slot_rows // count

    def saved_copies(s):
        return pltpu.make_async_copy(hidden_hbm.at[:, slots_ref[begin + s]], saved.at[:, s], saved_sem.at[s])

    @pl.when(expert == 0)
    def _():
        for copy in part_copies(parts, rows, part_sem):
            copy.start()
        each(count, lambda s: saved_copies(s).start())
        for copy in part_copies(parts, rows, part_sem):
            copy.wait()
        base = lax.axis_index("expert") * experts_here
        row, lane = iota((8, LANES), 0), iota((8, LANES), 1)
        wanted = base + jnp.where(row < experts_here, row, row - experts_here + LANES // 2)
        chosen = ((lane == wanted) & (row < 2 * experts_here)).astype(F32).astype(BF16)

        def look_up(s):
            at = pl.multiple_of(s * tokens, tokens)
            table_ref[s] = dot(chosen, rows[pl.ds(at, tokens), columns : columns + tokens])

        each(count, look_up)
        fill_slots(rows, routed, [table_ref], count)
        each(count, lambda s: saved_copies(s).wait())

    routed_ref[0] = routed[expert]
    if shares:
        product_ref[0] = dot(routed[expert], joined(weight_refs), ((1,), (1,))).astype(BF16)

    def weigh(s):
        hit, prob = hits(table_ref[s], expert, experts_here, cap)
        of_slot = jnp.sum(jnp.where(hit, prob, 0.0), axis=1, keepdims=True)
        scaled = of_slot * saved[expert, s].astype(F32)
        if cap_rows > cap:
            scaled = jnp.concatenate([scaled, jnp.zeros((cap_rows - cap, units), F32)], axis=0)
        weighted_ref[0, pl.ds(pl.multiple_of(s * cap_rows, cap_rows), cap_rows), :] = scaled.astype(BF16)

    each(count, weigh)


def visit(parts, slots, begin, weight, hidden, replicas, tokens, with_product=True):
    experts_here, _, cap, units = hidden.shape
    cap_rows = -(-cap // 16) * 16
    count = sum(part.shape[0] for part in parts) // tokens
    slot_rows = count * cap_rows
    columns = parts[0].shape[1] - tokens
    shares = weight_share(weight, columns, replicas, 0) if with_product else []
    product = jax.ShapeDtypeStruct((experts_here, slot_rows, units), BF16)
    routed = jax.ShapeDtypeStruct((experts_here, slot_rows, columns), BF16)
    table = jax.ShapeDtypeStruct((count, 8, tokens), F32)
    return pl.pallas_call(
        functools.partial(visit_kernel, len(parts), len(shares), begin),
        grid=(experts_here,),
        in_specs=[SMEM] + [HBM] * len(parts) + shares + [HBM],
        out_specs=[whole(routed), whole(product), pl.BlockSpec(table.shape, lambda e: (0, 0, 0))]
        + [whole(product)] * with_product,
        out_shape=[routed, product, table] + [product] * with_product,
        scratch_shapes=[
            pltpu.VMEM((count * tokens, parts[0].shape[1]), BF16),
            pltpu.VMEM((experts_here, slot_rows, columns), BF16),
            pltpu.VMEM((experts_here, count, cap, units), BF16),
            pltpu.SemaphoreType.DMA((len(parts),)),
            pltpu.SemaphoreType.DMA((count,)),
        ],
        compiler_params=params(),
        name="visit",
    )(slots, *parts, *[weight] * len(shares), hidden)


def owners(replicas):
    place = lax.axis_index("dp")
    groups = replicas // CORES
    chip, core = place // CORES, place % CORES
    away = [(chip + j + 1) % groups * CORES for j in range(groups)]
    return jnp.stack([at + 1 - core for at in away] + [at + core for at in away]).astype(jnp.int32)


def store_bands(taken, weighted_refs, outs):
    weighted = jnp.concatenate([ref[0] for ref in weighted_refs], axis=0)
    made = dot(taken, weighted, ((0,), (0,))).astype(BF16)
    at = 0
    for out_ref in outs:
        out_ref[...] = made[at : at + out_ref.shape[0], :]
        at += out_ref.shape[0]


def band_outputs(bands, width, experts_here, units, halves):
    rows = [len(band) * width for band in bands]
    if halves:
        rows = [rows[0] // 2, rows[0] // 2] + rows[1:]
    specs = [pl.BlockSpec((size, units), lambda e, *_: (0, e)) for size in rows]
    shapes = [jax.ShapeDtypeStruct((size, experts_here * units), BF16) for size in rows]
    return specs, shapes


def bands_kernel(total, groups_here, weighted_here, owners_ref, *refs):
    taken = [
        jnp.concatenate([ref[0] for ref in refs[j * groups_here : (j + 1) * groups_here]], axis=0)
        for j in range(total)
    ]
    refs = refs[total * groups_here :]
    store_bands(jnp.concatenate(taken, axis=1), refs[:weighted_here], refs[weighted_here:])


def grad_bands(routed, weighted, owned, bands, halves=True):
    experts_here, _, units = weighted[0].shape
    width = routed[0].shape[2] // owned.shape[0]
    wanted = [j for band in bands for j in band]
    out_specs, out_shape = band_outputs(bands, width, experts_here, units, halves)

    def share(part, j):
        return pl.BlockSpec((1, part.shape[1], width), lambda e, owned: (e, 0, owned[j]))

    return pl.pallas_call(
        functools.partial(bands_kernel, len(wanted), len(routed), len(weighted)),
        grid_spec=pltpu.PrefetchScalarGridSpec(
            num_scalar_prefetch=1,
            grid=(experts_here,),
            in_specs=[share(part, j) for j in wanted for part in routed] + [whole(part) for part in weighted],
            out_specs=out_specs,
        ),
        out_shape=out_shape,
        compiler_params=params(),
        name="bands",
    )(owned, *[part for _ in wanted for part in routed], *weighted)


def route_kernel(parts_here, groups_here, wanted, width, owners_ref, *refs):
    parts, refs = refs[:parts_here], refs[parts_here:]
    tables, refs = refs[:groups_here], refs[groups_here:]
    weighted, refs = refs[:groups_here], refs[groups_here:]
    outs, (routed_hbm, rows, routed, part_sem, out_sem) = refs[:-5], refs[-5:]
    expert = pl.program_id(0)
    keep = pltpu.make_async_copy(routed, routed_hbm, out_sem)

    @pl.when(expert == 0)
    def _():
        for copy in part_copies(parts, rows, part_sem):
            copy.start()
        for copy in part_copies(parts, rows, part_sem):
            copy.wait()
        fill_slots(rows, routed, tables, sum(table.shape[0] for table in tables))
        keep.start()

    taken = [routed[expert, :, pl.ds(pl.multiple_of(owners_ref[j] * width, LANES), width)] for j in wanted]
    store_bands(jnp.concatenate(taken, axis=1), weighted, outs)

    @pl.when(expert == pl.num_programs(0) - 1)
    def _():
        keep.wait()


def route(parts, tables, weighted, owned, bands):
    experts_here, _, units = weighted[0].shape
    slot_rows = sum(part.shape[1] for part in weighted)
    token_rows, tokens = sum(part.shape[0] for part in parts), tables[0].shape[2]
    columns = parts[0].shape[1]
    width = columns // owned.shape[0]
    out_specs, out_shape = band_outputs(bands, width, experts_here, units, True)
    wanted = [j for band in bands for j in band]
    return pl.pallas_call(
        functools.partial(route_kernel, len(parts), len(tables), wanted, width),
        grid=(experts_here,),
        in_specs=[SMEM]
        + [HBM] * len(parts)
        + [pl.BlockSpec(table.shape, lambda e: (0, 0, 0)) for table in tables]
        + [whole(part) for part in weighted],
        out_specs=out_specs + [HBM],
        out_shape=out_shape + [jax.ShapeDtypeStruct((experts_here, slot_rows, columns), BF16)],
        scratch_shapes=[
            pltpu.VMEM((token_rows, columns), BF16),
            pltpu.VMEM((experts_here, slot_rows, columns), BF16),
            pltpu.SemaphoreType.DMA((len(parts),)),
            pltpu.SemaphoreType.DMA,
        ],
        compiler_params=params(),
        cost_estimate=pl.CostEstimate(
            flops=2 * experts_here * slot_rows * columns * (units + tokens), bytes_accessed=10_000_000, transcendentals=0
        ),
        name="route",
    )(owned, *parts, *tables, *weighted)


def back_kernel(shares, seen_here, late_here, groups_here, slots_ref, routed_ref, *refs):
    last_weights, refs = refs[:shares], refs[shares:]
    first_weights, refs = refs[: shares * late_here], refs[shares * late_here :]
    late, refs = refs[:late_here], refs[late_here:]
    seen, refs = refs[:seen_here], refs[seen_here:]
    tables, refs = refs[:groups_here], refs[groups_here:]
    hidden_ref, grad_ref, prob_ref, held = refs
    expert = pl.program_id(0)
    experts_here = pl.num_programs(0)
    _, sources, cap, units = hidden_ref.shape
    cap_rows = held.shape[0] // sources
    before = [ref[0].astype(F32) for ref in seen]
    before += [dot(ref[0], joined(first_weights), ((1,), (1,))) for ref in late]
    held[...] = dot(routed_ref[0], joined(last_weights), ((1,), (1,))) + jnp.concatenate(before, axis=0)

    def finish(first, table_ref, s):
        at = first + s
        source = slots_ref[at]
        mine = held[pl.ds(pl.multiple_of(at * cap_rows, cap_rows), cap), :]
        hit, prob = hits(table_ref[s], expert, experts_here, cap)
        of_slot = jnp.sum(jnp.where(hit, prob, 0.0), axis=1, keepdims=True)
        grad_ref[0, pl.ds(source, 1)] = (of_slot * mine).astype(BF16)[None]
        inner = jnp.sum(mine * hidden_ref[0, source].astype(F32), axis=1, keepdims=True)
        gate = jnp.sum(jnp.where(hit, inner, 0.0), axis=0, keepdims=True)
        prob_ref[pl.ds(source, 1), pl.ds(expert, 1), :] = gate[None]

    first = 0
    for table_ref in tables:
        each(table_ref.shape[0], functools.partial(finish, first, table_ref))
        first += table_ref.shape[0]


def back(routed, slots, weight, hidden, start, replicas, seen, late, tables):
    experts_here, sources, cap, units = hidden.shape
    columns = routed.shape[2]
    tokens = tables[0].shape[2]
    saved = pl.BlockSpec((1, sources, cap, units), lambda e: (e, 0, 0, 0))
    return pl.pallas_call(
        functools.partial(back_kernel, replicas, len(seen), len(late), len(tables)),
        grid=(experts_here,),
        in_specs=[SMEM, whole(routed)]
        + weight_share(weight, columns, replicas, start)
        + weight_share(weight, columns, replicas, 0) * len(late)
        + [whole(part) for part in late]
        + [whole(part) for part in seen]
        + [pl.BlockSpec(table.shape, lambda e: (0, 0, 0)) for table in tables]
        + [saved],
        out_specs=[saved, pl.BlockSpec((sources, experts_here, tokens), lambda e: (0, 0, 0))],
        out_shape=[
            jax.ShapeDtypeStruct(hidden.shape, BF16),
            jax.ShapeDtypeStruct((sources, experts_here, tokens), F32),
        ],
        scratch_shapes=[pltpu.VMEM((routed.shape[1], units), F32)],
        compiler_params=params(),
        name="back",
    )(slots, routed, *[weight] * (replicas * (1 + len(late))), *late, *seen, *tables, hidden)


def rotate_kernel(count, experts_here, turn_ref, *refs):
    parts, out_ref = refs[:count], refs[-1]
    units = parts[0].shape[1] // experts_here
    total = parts[0][...].astype(F32)
    for ref in parts[1:]:
        total = total + ref[...].astype(F32)
    side = jnp.concatenate([total[:, e * units : (e + 1) * units] for e in range(experts_here)], axis=0)
    high = side.astype(BF16)
    low = (side - high.astype(F32)).astype(BF16)
    turn = turn_ref[0]
    turned = (dot(turn, high) + dot(turn, low)) * (1.0 / math.sqrt(BLOCK))
    out_ref[...] = turned.reshape(out_ref.shape)


def rotate(parts, turns, first_block, rows_out, experts_here, filled):
    rows, lines = parts[0].shape
    units = lines // experts_here
    extra = [] if filled is None else [filled]
    return pl.pallas_call(
        functools.partial(rotate_kernel, len(parts), experts_here),
        grid=(rows // BLOCK,),
        in_specs=[pl.BlockSpec((1,) + turns.shape[1:], lambda b: (first_block + b, 0, 0))]
        + [pl.BlockSpec((BLOCK, lines), lambda b: (b, 0)) for _ in parts]
        + [ANY] * len(extra),
        out_specs=pl.BlockSpec((BLOCK, experts_here, units), lambda b: (first_block + b, 0, 0)),
        out_shape=jax.ShapeDtypeStruct((rows_out, experts_here, units), F32),
        input_output_aliases={1 + len(parts): 0} if extra else {},
        compiler_params=params(),
        name="rotate",
    )(turns, *parts, *extra)


def turn_matrices(sign_seed, rows_own, experts_here):
    row = jnp.arange(BLOCK * experts_here, dtype=jnp.int32)
    anded = (row // experts_here)[:, None] & (row % BLOCK)[None, :]
    parity = sum(((anded >> shift) & 1) for shift in range(BLOCK.bit_length() - 1)) & 1
    same = (row % experts_here)[:, None] == (row // BLOCK)[None, :]
    matrix = jnp.where(same, 1 - 2 * parity, 0)
    own = lax.dynamic_slice_in_dim(2 * sign_seed - 1, lax.axis_index("dp") * rows_own, rows_own)
    signs = jnp.tile(own.reshape(-1, 1, BLOCK), (1, 1, experts_here))
    return (matrix[None] * signs).astype(BF16)


def shards(cotangent, gate_prob, routes, hidden, down_weight, sign_seed):
    tokens, features = cotangent.shape
    sources, replicas = lax.axis_size("expert"), lax.axis_size("dp")
    groups = replicas // CORES
    experts_here, units = down_weight.shape[0], down_weight.shape[1]
    rows_own = features // replicas
    saved = hidden[0]
    cap = saved.shape[2]
    width = rows_own // 2
    pieces = [(0, width), (width, width)]
    turns = turn_matrices(sign_seed, rows_own, experts_here)
    sent = pack(cotangent, gate_prob, routes, pieces, replicas)
    owned = owners(replicas)
    away_bands = [tuple(range(groups - 1)), tuple(range(groups, 2 * groups - 1))]
    here_bands = [(groups - 1,), (2 * groups - 1,)]

    def swap(value):
        return lax.ppermute(value, "dp", [(i, i ^ 1) for i in range(replicas)])

    def to_chips(value):
        moved = []
        for k in range(1, groups):
            pairs = [(i, (i // CORES + k) % groups * CORES + i % CORES) for i in range(replicas)]
            moved.append(lax.ppermute(value[(k - 1) * width : k * width], "dp", pairs))
        return moved

    def add_swapped(halves, kept):
        got = jnp.concatenate([swap(half) for half in halves], axis=0)
        return (got.astype(F32) + kept.astype(F32)).astype(BF16)

    def visit_first(parts, begin, with_product=True):
        return visit(parts, slots, begin, down_weight, saved, replicas, tokens, with_product)

    def bands_first(visits, bands, halves=True):
        return grad_bands([made[0] for made in visits], [made[1] for made in visits], owned, bands, halves)

    a, b = sent
    if sources == 2 * LINES:
        a_x, b_x, a_next, a_prev, a, b, turns, owned, slots = fence(
            across(a), across(b), along(a, 1), along(a, -1), a, b, turns, owned, line_slots()
        )
        a_opp, a_xnext, a_xprev = along(a, 2), across(a_next), across(a_prev)
        a_near = visit_first([a, a_x, a_next, a_prev], 0)
        a_opp, a_xnext, a_xprev, a_near, b = fence(a_opp, a_xnext, a_xprev, a_near, b)
        a_xopp, b_next, b_prev = across(a_opp), along(b, 1), along(b, -1)
        a_far = visit_first([a_opp, a_xnext, a_xprev], 4)
        a_xopp, a_far, b = fence(a_xopp, a_far, b)
        a_made = [a_near, a_far, visit_first([a_xopp], 7)]
        made = bands_first(a_made, away_bands)
        b_next, b_prev, made, b = fence(b_next, b_prev, made, b)
        b_opp, b_xnext, b_xprev = along(b, 2), across(b_next), across(b_prev)
        *away_send, away_keep = made
        here_send, here_keep = bands_first(a_made, here_bands, halves=False)
        b_opp, b_xnext, b_xprev, here_send, here_keep = fence(b_opp, b_xnext, b_xprev, here_send, here_keep)
        b_xopp = across(b_opp)
        a_arrived = to_chips(add_swapped(away_send, away_keep))
        b_xopp, here_send = fence(b_xopp, here_send)
        b_parts = [b, b_x, b_next, b_prev, b_opp, b_xnext, b_xprev, b_xopp]
        seen, late = [made[3] for made in a_made], []
    else:
        a, b = [lax.all_gather(part, "expert", axis=0, tiled=True) for part in sent]
        slots = jnp.arange(sources, dtype=jnp.int32)
        a_made = [visit_first([a], 0)]
        *away_send, away_keep, here_send, here_keep = bands_first(a_made, away_bands + here_bands)
        a_arrived = to_chips(add_swapped(away_send, away_keep))
        b_parts = [b]
        seen, late = [a_made[0][3]], []

    weighted = [made[1] for made in a_made]
    tables = [made[2] for made in a_made]
    made = route(b_parts, tables, weighted, owned, away_bands)
    made, a_arrived = fence(made, a_arrived)
    *away_send, away_keep, routed_b = made
    here_send_b, here_keep_b = grad_bands([routed_b], weighted, owned, here_bands, halves=False)
    b_arrived = to_chips(add_swapped(away_send, away_keep))
    here_got, here_got_b = swap(here_send), swap(here_send_b)
    grad_hidden, grad_slots = back(routed_b, slots, down_weight, saved, width, replicas, seen, late, tables)
    returned = lax.all_to_all(grad_slots, "expert", split_axis=0, concat_axis=0, tiled=True)
    out = rotate([here_keep, here_got] + a_arrived, turns, 0, rows_own, experts_here, None)
    out, *b_arrived = fence(out, *b_arrived)
    out = rotate([here_keep_b, here_got_b] + b_arrived, turns, width // BLOCK, rows_own, experts_here, out)
    returned, out = fence(returned, out)
    of_token = returned.reshape(-1, 1, tokens)
    named = routes.T[None] == jnp.arange(of_token.shape[0], dtype=jnp.int32)[:, None, None]
    grad_prob = jnp.sum(jnp.where(named, of_token, 0.0), axis=0)
    return (grad_hidden[None], grad_prob.T, out)


def solution(mesh):
    in_specs = (
        P(("dp", "expert"), None),
        P(("dp", "expert"), None),
        P(("dp", "expert"), None),
        P("dp", "expert", None, None, None),
        P("expert", None, None),
        P(),
    )
    out_specs = (
        P("dp", "expert", None, None, None),
        P(("dp", "expert"), None),
        P("dp", "expert", None),
    )
    return jax.shard_map(shards, mesh=mesh, in_specs=in_specs, out_specs=out_specs, check_vma=False)
```

```python
import functools
import math

import jax
import jax.numpy as jnp
from jax import lax
from jax.experimental import pallas as pl
from jax.experimental.pallas import tpu as pltpu
from jax.sharding import PartitionSpec as P

BLOCK = 128
LANES = 128
CORES = 2
NO_SLOT = 512.0
VMEM = 32 * 1024 * 1024
F32 = jnp.float32
BF16 = jnp.bfloat16


ANY = pl.BlockSpec(memory_space=pl.ANY)
HBM = pl.BlockSpec(memory_space=pltpu.HBM)
SMEM = pl.BlockSpec(memory_space=pltpu.SMEM)


def params(limit=VMEM):
    return pltpu.CompilerParams(vmem_limit_bytes=limit)


def dot(a, b, contract=((1,), (0,))):
    return lax.dot_general(a, b, (contract, ((), ())), preferred_element_type=F32)


def iota(shape, axis):
    return lax.broadcasted_iota(jnp.int32, shape, axis)


def pack_kernel(pieces, replicas, cot_ref, gate_ref, route_ref, *out_refs):
    rows_own = cot_ref.shape[1] // replicas
    for out_ref, (start, width) in zip(out_refs, pieces):
        for q in range(replicas):
            at = q * rows_own + start
            out_ref[:, q * width : (q + 1) * width] = cot_ref[:, at : at + width]
    tokens = cot_ref.shape[0]
    line = iota((LANES, tokens), 0)
    half = LANES // 2
    gate = jnp.zeros((LANES, tokens), F32)
    hit = jnp.zeros((LANES, tokens), F32)
    for k in range(route_ref.shape[0]):
        named = route_ref[k : k + 1, :]
        gate = gate + jnp.where(named == line, gate_ref[k : k + 1, :].astype(F32), 0.0)
        hit = hit + jnp.where(named == line - half, 1.0, 0.0)
    earlier = (iota((tokens, tokens), 0) < iota((tokens, tokens), 1)).astype(F32).astype(BF16)
    rank = dot(hit.astype(BF16), earlier)
    table = jnp.where(line < half, gate, jnp.where(hit > 0, rank, NO_SLOT))
    first = out_refs[0]
    first[:, first.shape[1] - tokens :] = table.astype(BF16)


def pack(cotangent, gate_prob, routes, pieces, replicas):
    tokens = cotangent.shape[0]
    widths = [replicas * width for _, width in pieces]
    widths[0] += tokens
    return pl.pallas_call(
        functools.partial(pack_kernel, pieces, replicas),
        out_shape=[jax.ShapeDtypeStruct((tokens, width), BF16) for width in widths],
        compiler_params=params(56 * 1024 * 1024),
        name="pack",
    )(cotangent, gate_prob.T, routes.T)


LINES = 4


def along(value, by):
    pairs = [(line, (line + by) % LINES) for line in range(LINES)]
    return lax.ppermute(value, "expert", [(2 * a + x, 2 * b + x) for a, b in pairs for x in (0, 1)])


def across(value):
    return lax.ppermute(value, "expert", [(i, i ^ 1) for i in range(2 * LINES)])


def fence(*values):
    return lax.optimization_barrier(values)


def line_slots():
    place = lax.axis_index("expert")
    line, side = place // 2, place % 2
    before, behind, facing = (line + LINES - 1) % LINES, (line + 1) % LINES, (line + 2) % LINES
    near = [2 * line + side, 2 * line + 1 - side, 2 * before + side, 2 * behind + side]
    far = [2 * facing + side, 2 * before + 1 - side, 2 * behind + 1 - side]
    farthest = [2 * facing + 1 - side]
    return jnp.stack(near + far + farthest).astype(jnp.int32)


def hits(table, expert, experts_here, cap_rows):
    line = iota(table.shape, 0)
    rank = jnp.sum(jnp.where(line == experts_here + expert, table, 0.0), axis=0, keepdims=True)
    prob = jnp.sum(jnp.where(line == expert, table, 0.0), axis=0, keepdims=True)
    return iota((cap_rows, table.shape[1]), 0).astype(F32) == rank, prob


def fill_slots(rows, routed, tables, sources):
    experts_here, slot_rows, columns = routed.shape
    cap_rows = slot_rows // sources
    tokens = rows.shape[0] // sources

    def fill(first, table_ref, s):
        table = table_ref[s]
        picked = [hits(table, e, experts_here, cap_rows)[0].astype(F32).astype(BF16) for e in range(experts_here)]
        at = pl.multiple_of((first + s) * tokens, tokens)
        got = dot(jnp.concatenate(picked, axis=0), rows[pl.ds(at, tokens), :columns]).astype(BF16)
        to = pl.multiple_of((first + s) * cap_rows, cap_rows)
        for e in range(experts_here):
            routed[e, pl.ds(to, cap_rows), :] = got[e * cap_rows : (e + 1) * cap_rows, :]

    first = 0
    for table_ref in tables:
        each(table_ref.shape[0], functools.partial(fill, first, table_ref))
        first += table_ref.shape[0]


def each(count, body):
    def step(s, carry):
        body(s)
        return carry

    lax.fori_loop(0, count, step, 0, unroll=count <= 8)


def part_copies(parts, rows, sem):
    size = rows.shape[0] // len(parts)
    return [
        pltpu.make_async_copy(part, rows.at[pl.ds(i * size, size), :], sem.at[i]) for i, part in enumerate(parts)
    ]


def whole(part):
    return pl.BlockSpec((1,) + part.shape[1:], lambda e, *_: (e, 0, 0))


def weight_share(weight, columns, replicas, start):
    units, features = weight.shape[1:]
    width, rows_own = columns // replicas, features // replicas

    def share(q):
        return pl.BlockSpec((1, units, width), lambda e: (e, 0, (q * rows_own + start) // width))

    return [share(q) for q in range(replicas)]


def joined(refs):
    return jnp.concatenate([ref[0] for ref in refs], axis=1)


def visit_kernel(parts_here, shares, begin, slots_ref, *refs):
    parts, refs = refs[:parts_here], refs[parts_here:]
    weight_refs, refs = refs[:shares], refs[shares:]
    hidden_hbm, routed_ref, weighted_ref, table_ref = refs[:4]
    product_ref = refs[4] if shares else None
    rows, routed, saved, part_sem, saved_sem = refs[-5:]
    expert = pl.program_id(0)
    experts_here, slot_rows, columns = routed.shape
    _, count, cap, units = saved.shape
    tokens = table_ref.shape[2]
    cap_rows = slot_rows // count

    def saved_copies(s):
        return pltpu.make_async_copy(hidden_hbm.at[:, slots_ref[begin + s]], saved.at[:, s], saved_sem.at[s])

    @pl.when(expert == 0)
    def _():
        for copy in part_copies(parts, rows, part_sem):
            copy.start()
        each(count, lambda s: saved_copies(s).start())
        for copy in part_copies(parts, rows, part_sem):
            copy.wait()
        base = lax.axis_index("expert") * experts_here
        row, lane = iota((8, LANES), 0), iota((8, LANES), 1)
        wanted = base + jnp.where(row < experts_here, row, row - experts_here + LANES // 2)
        chosen = ((lane == wanted) & (row < 2 * experts_here)).astype(F32).astype(BF16)

        def look_up(s):
            at = pl.multiple_of(s * tokens, tokens)
            table_ref[s] = dot(chosen, rows[pl.ds(at, tokens), columns : columns + tokens])

        each(count, look_up)
        fill_slots(rows, routed, [table_ref], count)
        each(count, lambda s: saved_copies(s).wait())

    routed_ref[0] = routed[expert]
    if shares:
        product_ref[0] = dot(routed[expert], joined(weight_refs), ((1,), (1,))).astype(BF16)

    def weigh(s):
        hit, prob = hits(table_ref[s], expert, experts_here, cap)
        of_slot = jnp.sum(jnp.where(hit, prob, 0.0), axis=1, keepdims=True)
        scaled = of_slot * saved[expert, s].astype(F32)
        if cap_rows > cap:
            scaled = jnp.concatenate([scaled, jnp.zeros((cap_rows - cap, units), F32)], axis=0)
        weighted_ref[0, pl.ds(pl.multiple_of(s * cap_rows, cap_rows), cap_rows), :] = scaled.astype(BF16)

    each(count, weigh)


def visit(parts, slots, begin, weight, hidden, replicas, tokens, with_product=True):
    experts_here, _, cap, units = hidden.shape
    cap_rows = -(-cap // 16) * 16
    count = sum(part.shape[0] for part in parts) // tokens
    slot_rows = count * cap_rows
    columns = parts[0].shape[1] - tokens
    shares = weight_share(weight, columns, replicas, 0) if with_product else []
    product = jax.ShapeDtypeStruct((experts_here, slot_rows, units), BF16)
    routed = jax.ShapeDtypeStruct((experts_here, slot_rows, columns), BF16)
    table = jax.ShapeDtypeStruct((count, 8, tokens), F32)
    return pl.pallas_call(
        functools.partial(visit_kernel, len(parts), len(shares), begin),
        grid=(experts_here,),
        in_specs=[SMEM] + [HBM] * len(parts) + shares + [HBM],
        out_specs=[whole(routed), whole(product), pl.BlockSpec(table.shape, lambda e: (0, 0, 0))]
        + [whole(product)] * with_product,
        out_shape=[routed, product, table] + [product] * with_product,
        scratch_shapes=[
            pltpu.VMEM((count * tokens, parts[0].shape[1]), BF16),
            pltpu.VMEM((experts_here, slot_rows, columns), BF16),
            pltpu.VMEM((experts_here, count, cap, units), BF16),
            pltpu.SemaphoreType.DMA((len(parts),)),
            pltpu.SemaphoreType.DMA((count,)),
        ],
        compiler_params=params(),
        name="visit",
    )(slots, *parts, *[weight] * len(shares), hidden)


def owners(replicas):
    place = lax.axis_index("dp")
    groups = replicas // CORES
    chip, core = place // CORES, place % CORES
    away = [(chip + j + 1) % groups * CORES for j in range(groups)]
    return jnp.stack([at + 1 - core for at in away] + [at + core for at in away]).astype(jnp.int32)


def store_bands(taken, weighted_refs, outs):
    weighted = jnp.concatenate([ref[0] for ref in weighted_refs], axis=0)
    made = dot(taken, weighted, ((0,), (0,))).astype(BF16)
    at = 0
    for out_ref in outs:
        out_ref[...] = made[at : at + out_ref.shape[0], :]
        at += out_ref.shape[0]


def band_outputs(bands, width, experts_here, units, halves):
    rows = [len(band) * width for band in bands]
    if halves:
        rows = [rows[0] // 2, rows[0] // 2] + rows[1:]
    specs = [pl.BlockSpec((size, units), lambda e, *_: (0, e)) for size in rows]
    shapes = [jax.ShapeDtypeStruct((size, experts_here * units), BF16) for size in rows]
    return specs, shapes


def bands_kernel(total, groups_here, weighted_here, owners_ref, *refs):
    taken = [
        jnp.concatenate([ref[0] for ref in refs[j * groups_here : (j + 1) * groups_here]], axis=0)
        for j in range(total)
    ]
    refs = refs[total * groups_here :]
    store_bands(jnp.concatenate(taken, axis=1), refs[:weighted_here], refs[weighted_here:])


def grad_bands(routed, weighted, owned, bands, halves=True):
    experts_here, _, units = weighted[0].shape
    width = routed[0].shape[2] // owned.shape[0]
    wanted = [j for band in bands for j in band]
    out_specs, out_shape = band_outputs(bands, width, experts_here, units, halves)

    def share(part, j):
        return pl.BlockSpec((1, part.shape[1], width), lambda e, owned: (e, 0, owned[j]))

    return pl.pallas_call(
        functools.partial(bands_kernel, len(wanted), len(routed), len(weighted)),
        grid_spec=pltpu.PrefetchScalarGridSpec(
            num_scalar_prefetch=1,
            grid=(experts_here,),
            in_specs=[share(part, j) for j in wanted for part in routed] + [whole(part) for part in weighted],
            out_specs=out_specs,
        ),
        out_shape=out_shape,
        compiler_params=params(),
        name="bands",
    )(owned, *[part for _ in wanted for part in routed], *weighted)


def route_kernel(parts_here, groups_here, wanted, width, owners_ref, *refs):
    parts, refs = refs[:parts_here], refs[parts_here:]
    tables, refs = refs[:groups_here], refs[groups_here:]
    weighted, refs = refs[:groups_here], refs[groups_here:]
    outs, (routed_hbm, rows, routed, part_sem, out_sem) = refs[:-5], refs[-5:]
    expert = pl.program_id(0)
    keep = pltpu.make_async_copy(routed, routed_hbm, out_sem)

    @pl.when(expert == 0)
    def _():
        for copy in part_copies(parts, rows, part_sem):
            copy.start()
        for copy in part_copies(parts, rows, part_sem):
            copy.wait()
        fill_slots(rows, routed, tables, sum(table.shape[0] for table in tables))
        keep.start()

    taken = [routed[expert, :, pl.ds(pl.multiple_of(owners_ref[j] * width, LANES), width)] for j in wanted]
    store_bands(jnp.concatenate(taken, axis=1), weighted, outs)

    @pl.when(expert == pl.num_programs(0) - 1)
    def _():
        keep.wait()


def route(parts, tables, weighted, owned, bands):
    experts_here, _, units = weighted[0].shape
    slot_rows = sum(part.shape[1] for part in weighted)
    token_rows, tokens = sum(part.shape[0] for part in parts), tables[0].shape[2]
    columns = parts[0].shape[1]
    width = columns // owned.shape[0]
    out_specs, out_shape = band_outputs(bands, width, experts_here, units, True)
    wanted = [j for band in bands for j in band]
    return pl.pallas_call(
        functools.partial(route_kernel, len(parts), len(tables), wanted, width),
        grid=(experts_here,),
        in_specs=[SMEM]
        + [HBM] * len(parts)
        + [pl.BlockSpec(table.shape, lambda e: (0, 0, 0)) for table in tables]
        + [whole(part) for part in weighted],
        out_specs=out_specs + [HBM],
        out_shape=out_shape + [jax.ShapeDtypeStruct((experts_here, slot_rows, columns), BF16)],
        scratch_shapes=[
            pltpu.VMEM((token_rows, columns), BF16),
            pltpu.VMEM((experts_here, slot_rows, columns), BF16),
            pltpu.SemaphoreType.DMA((len(parts),)),
            pltpu.SemaphoreType.DMA,
        ],
        compiler_params=params(),
        cost_estimate=pl.CostEstimate(
            flops=2 * experts_here * slot_rows * columns * (units + tokens), bytes_accessed=10_000_000, transcendentals=0
        ),
        name="route",
    )(owned, *parts, *tables, *weighted)


def back_kernel(shares, seen_here, late_here, groups_here, slots_ref, routed_ref, *refs):
    last_weights, refs = refs[:shares], refs[shares:]
    first_weights, refs = refs[: shares * late_here], refs[shares * late_here :]
    late, refs = refs[:late_here], refs[late_here:]
    seen, refs = refs[:seen_here], refs[seen_here:]
    tables, refs = refs[:groups_here], refs[groups_here:]
    hidden_ref, grad_ref, prob_ref, held = refs
    expert = pl.program_id(0)
    experts_here = pl.num_programs(0)
    _, sources, cap, units = hidden_ref.shape
    cap_rows = held.shape[0] // sources
    before = [ref[0].astype(F32) for ref in seen]
    before += [dot(ref[0], joined(first_weights), ((1,), (1,))) for ref in late]
    held[...] = dot(routed_ref[0], joined(last_weights), ((1,), (1,))) + jnp.concatenate(before, axis=0)

    def finish(first, table_ref, s):
        at = first + s
        source = slots_ref[at]
        mine = held[pl.ds(pl.multiple_of(at * cap_rows, cap_rows), cap), :]
        hit, prob = hits(table_ref[s], expert, experts_here, cap)
        of_slot = jnp.sum(jnp.where(hit, prob, 0.0), axis=1, keepdims=True)
        grad_ref[0, pl.ds(source, 1)] = (of_slot * mine).astype(BF16)[None]
        inner = jnp.sum(mine * hidden_ref[0, source].astype(F32), axis=1, keepdims=True)
        gate = jnp.sum(jnp.where(hit, inner, 0.0), axis=0, keepdims=True)
        prob_ref[pl.ds(source, 1), pl.ds(expert, 1), :] = gate[None]

    first = 0
    for table_ref in tables:
        each(table_ref.shape[0], functools.partial(finish, first, table_ref))
        first += table_ref.shape[0]


def back(routed, slots, weight, hidden, start, replicas, seen, late, tables):
    experts_here, sources, cap, units = hidden.shape
    columns = routed.shape[2]
    tokens = tables[0].shape[2]
    saved = pl.BlockSpec((1, sources, cap, units), lambda e: (e, 0, 0, 0))
    return pl.pallas_call(
        functools.partial(back_kernel, replicas, len(seen), len(late), len(tables)),
        grid=(experts_here,),
        in_specs=[SMEM, whole(routed)]
        + weight_share(weight, columns, replicas, start)
        + weight_share(weight, columns, replicas, 0) * len(late)
        + [whole(part) for part in late]
        + [whole(part) for part in seen]
        + [pl.BlockSpec(table.shape, lambda e: (0, 0, 0)) for table in tables]
        + [saved],
        out_specs=[saved, pl.BlockSpec((sources, experts_here, tokens), lambda e: (0, 0, 0))],
        out_shape=[
            jax.ShapeDtypeStruct(hidden.shape, BF16),
            jax.ShapeDtypeStruct((sources, experts_here, tokens), F32),
        ],
        scratch_shapes=[pltpu.VMEM((routed.shape[1], units), F32)],
        compiler_params=params(),
        name="back",
    )(slots, routed, *[weight] * (replicas * (1 + len(late))), *late, *seen, *tables, hidden)


def rotate_kernel(count, experts_here, turn_ref, *refs):
    parts, out_ref = refs[:count], refs[-1]
    units = parts[0].shape[1] // experts_here
    total = parts[0][...].astype(F32)
    for ref in parts[1:]:
        total = total + ref[...].astype(F32)
    side = jnp.concatenate([total[:, e * units : (e + 1) * units] for e in range(experts_here)], axis=0)
    high = side.astype(BF16)
    low = (side - high.astype(F32)).astype(BF16)
    turn = turn_ref[0]
    turned = (dot(turn, high) + dot(turn, low)) * (1.0 / math.sqrt(BLOCK))
    out_ref[...] = turned.reshape(out_ref.shape)


def rotate(parts, turns, first_block, rows_out, experts_here, filled):
    rows, lines = parts[0].shape
    units = lines // experts_here
    extra = [] if filled is None else [filled]
    return pl.pallas_call(
        functools.partial(rotate_kernel, len(parts), experts_here),
        grid=(rows // BLOCK,),
        in_specs=[pl.BlockSpec((1,) + turns.shape[1:], lambda b: (first_block + b, 0, 0))]
        + [pl.BlockSpec((BLOCK, lines), lambda b: (b, 0)) for _ in parts]
        + [ANY] * len(extra),
        out_specs=pl.BlockSpec((BLOCK, experts_here, units), lambda b: (first_block + b, 0, 0)),
        out_shape=jax.ShapeDtypeStruct((rows_out, experts_here, units), F32),
        input_output_aliases={1 + len(parts): 0} if extra else {},
        compiler_params=params(),
        name="rotate",
    )(turns, *parts, *extra)


def turn_matrices(sign_seed, rows_own, experts_here):
    row = jnp.arange(BLOCK * experts_here, dtype=jnp.int32)
    anded = (row // experts_here)[:, None] & (row % BLOCK)[None, :]
    parity = sum(((anded >> shift) & 1) for shift in range(BLOCK.bit_length() - 1)) & 1
    same = (row % experts_here)[:, None] == (row // BLOCK)[None, :]
    matrix = jnp.where(same, 1 - 2 * parity, 0)
    own = lax.dynamic_slice_in_dim(2 * sign_seed - 1, lax.axis_index("dp") * rows_own, rows_own)
    signs = jnp.tile(own.reshape(-1, 1, BLOCK), (1, 1, experts_here))
    return (matrix[None] * signs).astype(BF16)


def shards(cotangent, gate_prob, routes, hidden, down_weight, sign_seed):
    tokens, features = cotangent.shape
    sources, replicas = lax.axis_size("expert"), lax.axis_size("dp")
    groups = replicas // CORES
    experts_here, units = down_weight.shape[0], down_weight.shape[1]
    rows_own = features // replicas
    saved = hidden[0]
    cap = saved.shape[2]
    width = rows_own // 2
    pieces = [(0, width), (width, width)]
    turns = turn_matrices(sign_seed, rows_own, experts_here)
    sent = pack(cotangent, gate_prob, routes, pieces, replicas)
    owned = owners(replicas)
    away_bands = [tuple(range(groups - 1)), tuple(range(groups, 2 * groups - 1))]
    here_bands = [(groups - 1,), (2 * groups - 1,)]

    def swap(value):
        return lax.ppermute(value, "dp", [(i, i ^ 1) for i in range(replicas)])

    def to_chips(value):
        moved = []
        for k in range(1, groups):
            pairs = [(i, (i // CORES + k) % groups * CORES + i % CORES) for i in range(replicas)]
            moved.append(lax.ppermute(value[(k - 1) * width : k * width], "dp", pairs))
        return moved

    def add_swapped(halves, kept):
        got = jnp.concatenate([swap(half) for half in halves], axis=0)
        return (got.astype(F32) + kept.astype(F32)).astype(BF16)

    def visit_first(parts, begin, with_product=True):
        return visit(parts, slots, begin, down_weight, saved, replicas, tokens, with_product)

    def bands_first(visits, bands, halves=True):
        return grad_bands([made[0] for made in visits], [made[1] for made in visits], owned, bands, halves)

    a, b = sent
    if sources == 2 * LINES:
        a_x, b_x, a_next, a_prev, a, b, turns, owned, slots = fence(
            across(a), across(b), along(a, 1), along(a, -1), a, b, turns, owned, line_slots()
        )
        a_opp, a_xnext, a_xprev = along(a, 2), across(a_next), across(a_prev)
        a_near = visit_first([a, a_x, a_next, a_prev], 0)
        a_opp, a_xnext, a_xprev, a_near, b = fence(a_opp, a_xnext, a_xprev, a_near, b)
        a_xopp, b_next, b_prev = across(a_opp), along(b, 1), along(b, -1)
        a_far = visit_first([a_opp, a_xnext, a_xprev], 4)
        a_xopp, a_far, b = fence(a_xopp, a_far, b)
        a_made = [a_near, a_far, visit_first([a_xopp], 7)]
        made = bands_first(a_made, away_bands)
        b_next, b_prev, made, b = fence(b_next, b_prev, made, b)
        b_opp, b_xnext, b_xprev = along(b, 2), across(b_next), across(b_prev)
        *away_send, away_keep = made
        here_send, here_keep = bands_first(a_made, here_bands, halves=False)
        b_opp, b_xnext, b_xprev, here_send, here_keep = fence(b_opp, b_xnext, b_xprev, here_send, here_keep)
        b_xopp = across(b_opp)
        a_arrived = to_chips(add_swapped(away_send, away_keep))
        b_xopp, here_send = fence(b_xopp, here_send)
        b_parts = [b, b_x, b_next, b_prev, b_opp, b_xnext, b_xprev, b_xopp]
        seen, late = [made[3] for made in a_made], []
    else:
        a, b = [lax.all_gather(part, "expert", axis=0, tiled=True) for part in sent]
        slots = jnp.arange(sources, dtype=jnp.int32)
        a_made = [visit_first([a], 0)]
        *away_send, away_keep, here_send, here_keep = bands_first(a_made, away_bands + here_bands)
        a_arrived = to_chips(add_swapped(away_send, away_keep))
        b_parts = [b]
        seen, late = [a_made[0][3]], []

    weighted = [made[1] for made in a_made]
    tables = [made[2] for made in a_made]
    made = route(b_parts, tables, weighted, owned, away_bands[:1])
    made, a_arrived = fence(made, a_arrived)
    *away_send, routed_b = made
    (away_keep,) = grad_bands([routed_b], weighted, owned, away_bands[1:], halves=False)
    here_send_b, here_keep_b = grad_bands([routed_b], weighted, owned, here_bands, halves=False)
    b_arrived = to_chips(add_swapped(away_send, away_keep))
    here_got, here_got_b = swap(here_send), swap(here_send_b)
    grad_hidden, grad_slots = back(routed_b, slots, down_weight, saved, width, replicas, seen, late, tables)
    returned = lax.all_to_all(grad_slots, "expert", split_axis=0, concat_axis=0, tiled=True)
    out = rotate([here_keep, here_got] + a_arrived, turns, 0, rows_own, experts_here, None)
    out, *b_arrived = fence(out, *b_arrived)
    out = rotate([here_keep_b, here_got_b] + b_arrived, turns, width // BLOCK, rows_own, experts_here, out)
    returned, out = fence(returned, out)
    of_token = returned.reshape(-1, 1, tokens)
    named = routes.T[None] == jnp.arange(of_token.shape[0], dtype=jnp.int32)[:, None, None]
    grad_prob = jnp.sum(jnp.where(named, of_token, 0.0), axis=0)
    return (grad_hidden[None], grad_prob.T, out)


def solution(mesh):
    in_specs = (
        P(("dp", "expert"), None),
        P(("dp", "expert"), None),
        P(("dp", "expert"), None),
        P("dp", "expert", None, None, None),
        P("expert", None, None),
        P(),
    )
    out_specs = (
        P("dp", "expert", None, None, None),
        P(("dp", "expert"), None),
        P("dp", "expert", None),
    )
    return jax.shard_map(shards, mesh=mesh, in_specs=in_specs, out_specs=out_specs, check_vma=False)
```
